512 devices in a mesh: dp: 64 (over x, z, core), tensor: 8 (over y).
Axes of the slice: x: 4, y: 8, z: 8, core: 2. Of those that a mesh axis runs over, the one named last changes fastest.
Arguments:
- acts: bfloat16 [8192, 3072], P('dp', 'tensor'), may hold values from -6 to 6
- grads_out: bfloat16 [8192, 3072], P('dp', 'tensor'), may hold values from -1.5 to 1.5
- weight: bfloat16 [3072, 3072], P('dp', 'tensor'), may hold values from -0.109375 to 0.109375
- basis_init: float32 [64, 3072], P(None, 'tensor'), may hold values from -6 to 6
- feedback: bfloat16 [64, 3072, 3072], P('dp', None, 'tensor'), may hold values from -8 to 8
Outputs:
- input_grads: bfloat16 [8192, 3072], P('dp', 'tensor')
- new_feedback: bfloat16 [64, 3072, 3072], P('dp', None, 'tensor')
- update: float32 [3072, 3072], P('dp', 'tensor')
The draws below stay inside these ranges and needn't reach their ends.
All inputs are finite; a program needn't handle non-finite values.
Results may differ from the reference program's by a relative error of at most 0.00055.
Values may be sent and summed in bfloat16 or wider, within the bound.
A program may use at most 64 MiB of HBM per device.

```python
import jax
import jax.numpy as jnp
from jax import lax

D = 3072
RANK = 64
TOK_DEV = 128
HD = 3072
TOKENS = 8192
N_DP = 64
N_TENSOR = 8


def strengthened(drawn, own_key, source, target, shards_of, factor):
    def block_of(axis_at):
        return (jnp.arange(drawn.shape[axis_at]) // (drawn.shape[axis_at] // shards_of)).reshape((-1,) + (1,) * (drawn.ndim - 1 - axis_at))

    near = jax.random.permutation(own_key, shards_of)[block_of(target)]
    far = (block_of(target) + shards_of // 2) % shards_of
    return jnp.where((block_of(source) == near) | (block_of(source) == far), factor * drawn, drawn)


def shard_levels(own_key, dims, pieces, least, top_value):
    def one(position, parts):
        steps = jax.random.uniform(jax.random.fold_in(jax.random.fold_in(own_key, 6), position), (parts,), jnp.float32, least / len(pieces), top_value / len(pieces))
        return jnp.repeat(jnp.exp(steps), dims[position] // parts).reshape((-1,) + (1,) * (len(dims) - position - 1))

    level = one(*pieces[0])
    for cut in pieces[1:]:
        level = level * one(*cut)
    return level


def gaussian(own_key, shape, spread, reach, split=(), kind=jnp.bfloat16):
    factor_of = shard_levels(own_key, shape, split, -0.22, 0.18) if split else 1.0
    result = jax.random.normal(own_key, shape, jnp.float32) * spread * factor_of
    return jnp.minimum(jnp.maximum(result, -reach), reach).astype(kind)


def bell_draw_with(rng, dims, width, most, split, heavy, kind=jnp.bfloat16):
    entries = width * jax.random.normal(rng, dims, jnp.float32)
    if split:
        entries = entries * shard_levels(rng, dims, split, -0.22, 0.18)
    return jnp.clip(strengthened(entries, jax.random.fold_in(rng, 3), *heavy), -most, most).astype(kind)


def setup_inputs(seed: int = 0) -> dict:
    splits = jax.random.split(jax.random.key(seed), 6)
    acts = gaussian(splits[0], (TOKENS, D), 1.0, 6.0, ((0, 64), (1, 8)))
    grads_out = gaussian(splits[1], (TOKENS, HD), 0.25, 1.5, ((0, 64), (1, 8)))
    weight = gaussian(splits[2], (D, HD), D ** -0.5, 0.109375, ((0, 64), (1, 8)))
    basis_init = gaussian(splits[3], (RANK, HD), 1.0, 6.0, ((1, 8),), jnp.float32)
    feedback = bell_draw_with(splits[4], (N_DP, D, HD), 1.0, 8.0, ((0, 64), (2, 8)), (0, 1, 64, 4.0))
    return dict(acts=acts, grads_out=grads_out, weight=weight, basis_init=basis_init, feedback=feedback)


def contribution(acts, grads_out, feedback, index):
    start = index * TOK_DEV
    rows_in = lax.dynamic_slice_in_dim(acts, start, TOK_DEV, 0)
    rows_out = lax.dynamic_slice_in_dim(grads_out, start, TOK_DEV, 0)
    gradient = jnp.dot(rows_in.T.astype(jnp.float32), rows_out.astype(jnp.float32), preferred_element_type=jnp.float32)
    return gradient + feedback[index].astype(jnp.float32)

def reference(acts, grads_out, weight, basis_init, feedback):
    highest = lax.Precision.HIGHEST
    group = HD // N_TENSOR
    input_grads = jnp.dot(grads_out.astype(jnp.float32), weight.T.astype(jnp.float32), preferred_element_type=jnp.float32).astype(jnp.bfloat16)
    basis_groups = basis_init.reshape(RANK, N_TENSOR, group)
    indices = jnp.arange(N_DP, dtype=jnp.int32)

    def first_pass(carry, index):
        total_grad = contribution(acts, grads_out, feedback, index).reshape(D, N_TENSOR, group)
        return (carry + jnp.einsum('rtk,dtk->trd', basis_groups, total_grad, precision=highest), None)
    factor, _ = lax.scan(first_pass, jnp.zeros((N_TENSOR, RANK, D), jnp.float32), indices)
    gram_matrix = jnp.einsum('trd,tsd->trs', factor, factor, precision=highest)
    cholesky_factor = jnp.linalg.cholesky(gram_matrix)
    orth_basis = lax.linalg.triangular_solve(cholesky_factor, factor, left_side=True, lower=True)

    def second_pass(carry, index):
        total_grad = contribution(acts, grads_out, feedback, index).reshape(D, N_TENSOR, group)
        return (carry + jnp.einsum('trd,dtk->trk', orth_basis, total_grad, precision=highest), None)
    second, _ = lax.scan(second_pass, jnp.zeros((N_TENSOR, RANK, group), jnp.float32), indices)
    update = jnp.einsum('trd,trk->dtk', orth_basis, second, precision=highest).reshape(D, HD) / N_DP

    def third_pass(index):
        return (contribution(acts, grads_out, feedback, index) - update).astype(jnp.bfloat16)
    new_feedback = lax.map(third_pass, indices)
    return (input_grads, new_feedback, update)
```

```python
import jax
import jax.numpy as jnp
from jax import lax
from jax.experimental import pallas as pl
from jax.experimental.pallas import tpu as pltpu
from jax.sharding import PartitionSpec as P

MESH = pl.DeviceIdType.MESH
F32 = jnp.float32
BF16 = jnp.bfloat16
RANK = 64
TOK = 128
WIDTH = 384
NT = 8
NX, NZ, NC = 4, 8, 2
ROWS = 48
D = NT * WIDTH

NN = (((1,), (0,)), ((), ()))
NTD = (((1,), (1,)), ((), ()))
TN = (((0,), (0,)), ((), ()))


def mm(a, b, dims):
    return lax.dot_general(a, b, dims, preferred_element_type=F32)


def mm32(a, b, dims):
    return lax.dot_general(
        a, b, dims, precision=lax.Precision.HIGHEST, preferred_element_type=F32
    )


def pieces(value, n):
    parts = []
    for _ in range(n):
        top = value.astype(BF16)
        parts.append(top)
        value = value - top.astype(F32)
    return jnp.concatenate(parts, axis=0)


def folded(stack, n):
    rows = stack.shape[0] // n
    total = stack[(n - 1) * rows :]
    for i in range(n - 2, -1, -1):
        total = total + stack[i * rows : (i + 1) * rows]
    return total


def eliminate(a, first, last):
    rows = lax.broadcasted_iota(jnp.int32, (RANK, 1), 0)
    for j in range(first, last):
        scaled = a[j : j + 1, :] / a[j : j + 1, j : j + 1]
        column = jnp.where(rows > j, a[:, j : j + 1], 0.0)
        a = a - column * scaled
    return a


def kernel(
    acts, grads, weight, basis, fb_hbm,
    ig_out, nf_out, up_out,
    fb, acts_all, grads_all, wbuf, fp, rc, f1, rx, f2, rz, f_all, ft, t0, nf,
    sp, rs, rsz, sfull,
    fb_sem, nf_sem,
    ring_s, ring_r, gr_s, gr_r, spread_s, spread_r, wz_s, wz_r, wx_s, wx_r, wc_s, wc_r,
    fc_s, fc_r, fx_s, fx_r, fz_s, fz_r, az_s, az_r, ax_s, ax_r, ac_s, ac_r,
    sx_s, sx_r, sz_s, sz_r, sa_s, sa_r,
):
    dp = lax.axis_index("dp")
    y = lax.axis_index("tensor")
    c = dp % NC
    z = (dp // NC) % NZ
    x = dp // (NC * NZ)

    def at(x_, z_, c_):
        return (x_ * NZ + z_) * NC + c_

    q = c * NX + x
    group = dp // NT
    pair_dp = y * NT + dp % NT
    y_peers = [(dp, (y + k) % NT) for k in range(1, NT)]
    z_peers = [(at(x, (z + k) % NZ, c), y) for k in range(1, NZ)]
    xc_peers = [
        (at((x + (o % NX)) % NX, z, (c + o // NX) % NC), y) for o in range(1, NX * NC)
    ]
    partner = xc_peers[NX - 1]
    x_peers = xc_peers[: NX - 1]
    swaps = group != y

    sends = []

    def send(src, dst, ssem, rsem, peer):
        cp = pltpu.make_async_remote_copy(
            src_ref=src, dst_ref=dst, send_sem=ssem, recv_sem=rsem,
            device_id=peer, device_id_type=MESH,
        )
        cp.start()
        sends.append(cp)
        return cp

    barrier = pltpu.get_barrier_semaphore()
    for peer in y_peers + z_peers + xc_peers:
        pl.semaphore_signal(barrier, inc=1, device_id=peer, device_id_type=MESH)

    @pl.when(swaps)
    def _():
        pl.semaphore_signal(barrier, inc=1, device_id=(pair_dp, group), device_id_type=MESH)

    load = pltpu.make_async_copy(fb_hbm.at[0], fb, fb_sem)
    load.start()
    acts_all[y] = acts[...]
    grads_all[y] = grads[...]
    pl.semaphore_wait(barrier, 21 + jnp.where(swaps, 1, 0))

    right = (dp, (y + 1) % NT)
    left = (dp, (y + NT - 1) % NT)
    half = TOK // 2

    def ring(way, k, h, peer):
        slot = (y - k + NT) % NT if way == 0 else (y + k) % NT
        part = acts_all.at[slot, pl.ds(h * half, half)]
        return send(part, part, ring_s.at[way, k, h], ring_r.at[way, k, h], peer)

    hops = {}
    for h in range(2):
        hops[0, 0, h] = ring(0, 0, h, right)
        hops[1, 0, h] = ring(1, 0, h, left)

    bh, bc = (dp % NT) // NC, c
    mine = wbuf.at[group, bh, bc]
    swap = pltpu.make_async_remote_copy(
        src_ref=weight, dst_ref=wbuf.at[y, bh, bc], send_sem=spread_s, recv_sem=spread_r,
        device_id=(pair_dp, group), device_id_type=MESH,
    )

    @pl.when(swaps)
    def _():
        swap.start()

    @pl.when(jnp.logical_not(swaps))
    def _():
        wbuf[group, bh, bc] = weight[...]

    bs = pieces(basis[...], 3)
    hs = pieces(folded(mm(bs, grads[...], NTD), 3), 3)
    load.wait()
    for t in range(NT):
        fp[t] = folded(mm(bs, fb[t * WIDTH : (t + 1) * WIDTH], NTD), 3)

    core_cp, x_cp = {}, {}

    def block_of(k, way):
        return (y - k + NT) % NT if way == 0 else (y + k) % NT

    def add_acts(k, way):
        t = block_of(k, way)
        fp[t] = fp[t] + folded(mm(hs, acts_all[t], NN), 3)
        core_cp[k, way] = send(
            fp.at[t, pl.ds(32 * (1 - c), 32)], rc.at[t], fc_s.at[t], fc_r.at[t], partner
        )

    def x_stage(k, way):
        t = block_of(k, way)
        core_cp[k, way].wait_recv()
        f1[t] = fp[t, pl.ds(pl.multiple_of(32 * c, 32), 32)] + rc[t]
        for d in range(1, NX):
            to = (x + d) % NX
            x_cp[k, way, d] = send(
                f1.at[t, pl.ds(pl.multiple_of(8 * to, 8), 8)], rx.at[d - 1, t],
                fx_s.at[d - 1, t], fx_r.at[d - 1, t], x_peers[d - 1],
            )

    ways = {0: [0], 1: [0, 1], 2: [0, 1], 3: [0, 1], 4: [0]}
    for k in range(5):
        if k:
            for h in range(2):
                for way, peer in ((0, right), (1, left)):
                    if (way, k - 1, h) in hops:
                        hops[way, k - 1, h].wait_recv()
                        if k < 3 or (k == 3 and h == way):
                            hops[way, k, h] = ring(way, k, h, peer)
        for way in ways[k]:
            add_acts(k, way)
        if k == 1:
            @pl.when(swaps)
            def _():
                swap.wait()
            wz = [
                send(mine, mine, wz_s.at[i], wz_r.at[i], z_peers[i]) for i in range(NZ - 1)
            ]
        if k:
            for way in ways[k - 1]:
                x_stage(k - 1, way)

    gcp = [
        send(grads, grads_all.at[y], gr_s.at[i], gr_r.at[i], y_peers[i])
        for i in range(NT - 1)
    ]
    x_stage(4, 0)
    for t in range(NT):
        rows = pl.ds(t * WIDTH, WIDTH)
        t0[rows] = mm(acts_all[t], grads[...], TN) + fb[rows].astype(F32)
    for key in x_cp:
        x_cp[key].wait_recv()
    own = pl.ds(pl.multiple_of(8 * x, 8), 8)
    for t in range(NT):
        f2[t] = f1[t, own] + rx[0, t] + rx[1, t] + rx[2, t]
    fz = [
        send(f2.at[(z + i + 1) % NZ], rz.at[i], fz_s.at[i], fz_r.at[i], z_peers[i])
        for i in range(NZ - 1)
    ]
    for cp in wz:
        cp.wait_recv()
    wmine = wbuf.at[pl.ds(2 * x, 2), :, c]
    wx = [send(wmine, wmine, wx_s.at[i], wx_r.at[i], x_peers[i]) for i in range(NX - 1)]
    f3 = f2[z]
    for i in range(NZ - 1):
        fz[i].wait_recv()
        f3 = f3 + rz[i]

    top = f3.astype(BF16).astype(F32)
    f_all[z, q] = jnp.concatenate([top, f3 - top], axis=0).astype(BF16)
    az = [
        send(f_all.at[z, q], f_all.at[z, q], az_s.at[i], az_r.at[i], z_peers[i])
        for i in range(NZ - 1)
    ]
    for cp in az:
        cp.wait_recv()
    ax = [
        send(f_all.at[:, q], f_all.at[:, q], ax_s.at[i], ax_r.at[i], x_peers[i])
        for i in range(NX - 1)
    ]
    for cp in ax:
        cp.wait_recv()
    core_half = f_all.at[:, pl.ds(NX * c, NX)]
    ac = send(core_half, core_half, ac_s, ac_r, partner)
    ac.wait_recv()

    def unpaired(pairs):
        v = pairs.reshape(RANK // 8, 2, 8, pairs.shape[1])
        return (v[:, 0] + v[:, 1]).reshape(RANK, pairs.shape[1])

    through = jnp.zeros((2 * RANK, TOK), F32)
    direct = jnp.zeros((2 * RANK, WIDTH), F32)
    for t in range(NT):
        block = f_all[t].reshape(2 * RANK, WIDTH)
        through = through + mm(block, acts_all[t], NTD)
        direct = direct + mm(block, fb[t * WIDTH : (t + 1) * WIDTH], NN)
    local = unpaired(direct) + folded(mm(pieces(unpaired(through), 3), grads[...], NN), 3)
    sp[...] = local.reshape(RANK // 8, 8, WIDTH)
    sx = []
    for o in range(1, NX * NC):
        to = ((c + o // NX) % NC) * NX + (x + o % NX) % NX
        sx.append(
            send(sp.at[to], rs.at[o - 1], sx_s.at[o - 1], sx_r.at[o - 1], xc_peers[o - 1])
        )

    gram = jnp.zeros((2 * RANK, 2 * RANK), F32)
    for t in range(NT):
        block = f_all[t].reshape(2 * RANK, WIDTH)
        gram = gram + mm(block, block, NTD)
    lanes = lax.broadcasted_iota(jnp.int32, (2 * RANK, RANK), 0)
    cols = lax.broadcasted_iota(jnp.int32, (2 * RANK, RANK), 1)
    pick = jnp.where((lanes // 16) * 8 + lanes % 8 == cols, 1.0, 0.0)
    gram = mm32(unpaired(gram), pick, NN)
    eye = jnp.where(
        lax.broadcasted_iota(jnp.int32, (RANK, RANK), 0)
        == lax.broadcasted_iota(jnp.int32, (RANK, RANK), 1), 1.0, 0.0,
    )
    a = jnp.concatenate([gram, eye], axis=1)
    a = eliminate(a, 0, 12)

    s1 = sp[q]
    for i in range(NX * NC - 1):
        sx[i].wait_recv()
        s1 = s1 + rs[i]
    rsz[z] = s1
    sz = [
        send(rsz.at[z], rsz.at[z], sz_s.at[i], sz_r.at[i], z_peers[i]) for i in range(NZ - 1)
    ]
    a = eliminate(a, 12, 44)
    for cp in sz:
        cp.wait_recv()
    s2 = rsz[0]
    for i in range(1, NZ):
        s2 = s2 + rsz[i]
    sfull[q] = s2
    sa = [
        send(sfull.at[q], sfull.at[q], sa_s.at[i], sa_r.at[i], xc_peers[i])
        for i in range(NX * NC - 1)
    ]
    a = eliminate(a, 44, RANK)
    for t in range(NT):
        ft[pl.ds(t * WIDTH, WIDTH)] = (
            f_all[t].reshape(2 * RANK, WIDTH).astype(F32).T.astype(BF16)
        )
    pivots = jnp.sum(a[:, :RANK] * eye, axis=1, keepdims=True)
    inverse = a[:, RANK:]
    for cp in wx:
        cp.wait_recv()
    whalf = wbuf.at[:, :, c]
    wc = send(whalf, whalf, wc_s, wc_r, partner)
    for cp in sa:
        cp.wait_recv()

    solved = mm32(inverse, sfull[...].reshape(RANK, WIDTH), NN) / (pivots * 64.0)
    coef = mm32(inverse, solved, TN)
    ctop = coef.astype(BF16).astype(F32)

    def doubled(v):
        v = v.reshape(RANK // 8, 1, 8, WIDTH)
        return jnp.concatenate([v, v], axis=1).reshape(2 * RANK, WIDTH).astype(BF16)

    c1, c2 = doubled(ctop), doubled(coef - ctop)

    def low_rank(rows):
        left_side = ft[rows]
        return mm(left_side, c1, NN) + mm(left_side, c2, NN)

    stores = []
    for t in range(NT):
        rows = pl.ds(t * WIDTH, WIDTH)
        nf[rows] = (t0[rows] - low_rank(rows)).astype(BF16)
        cp = pltpu.make_async_copy(nf.at[rows], nf_out.at[0, rows], nf_sem.at[t])
        cp.start()
        stores.append(cp)
    up_out[...] = low_rank(pl.ds(pl.multiple_of(dp * ROWS, 16), ROWS))

    for cp in gcp:
        cp.wait_recv()
    wc.wait_recv()
    out = jnp.zeros((TOK, WIDTH), F32)
    for j in range(NT):
        out = out + mm(grads_all[j], wbuf[j].reshape(WIDTH, WIDTH), NTD)
    ig_out[...] = out.astype(BF16)

    for cp in stores:
        cp.wait()
    for cp in sends:
        cp.wait_send()


def local(acts, grads_out, weight, basis_init, feedback):
    vmem = pl.BlockSpec(memory_space=pltpu.VMEM)
    hbm = pl.BlockSpec(memory_space=pl.ANY)
    dma = pltpu.SemaphoreType.DMA
    scratch = [
        pltpu.VMEM((D, WIDTH), BF16),
        pltpu.VMEM((NT, TOK, WIDTH), BF16),
        pltpu.VMEM((NT, TOK, WIDTH), BF16),
        pltpu.VMEM((NT, 4, NC, ROWS, WIDTH), BF16),
        pltpu.VMEM((NT, RANK, WIDTH), F32),
        pltpu.VMEM((NT, RANK // 2, WIDTH), F32),
        pltpu.VMEM((NT, RANK // 2, WIDTH), F32),
        pltpu.VMEM((NX - 1, NT, 8, WIDTH), F32),
        pltpu.VMEM((NT, 8, WIDTH), F32),
        pltpu.VMEM((NZ - 1, 8, WIDTH), F32),
        pltpu.VMEM((NT, NX * NC, 16, WIDTH), BF16),
        pltpu.VMEM((D, 2 * RANK), BF16),
        pltpu.VMEM((D, WIDTH), F32),
        pltpu.VMEM((D, WIDTH), BF16),
        pltpu.VMEM((NX * NC, 8, WIDTH), F32),
        pltpu.VMEM((NX * NC - 1, 8, WIDTH), F32),
        pltpu.VMEM((NZ, 8, WIDTH), F32),
        pltpu.VMEM((NX * NC, 8, WIDTH), F32),
        dma, dma((NT,)),
        dma((2, 4, 2)), dma((2, 4, 2)),
        dma((NT - 1,)), dma((NT - 1,)),
        dma, dma,
        dma((NZ - 1,)), dma((NZ - 1,)),
        dma((NX - 1,)), dma((NX - 1,)),
        dma, dma,
        dma((NT,)), dma((NT,)),
        dma((NX - 1, NT)), dma((NX - 1, NT)),
        dma((NZ - 1,)), dma((NZ - 1,)),
        dma((NZ - 1,)), dma((NZ - 1,)),
        dma((NX - 1,)), dma((NX - 1,)),
        dma, dma,
        dma((NX * NC - 1,)), dma((NX * NC - 1,)),
        dma((NZ - 1,)), dma((NZ - 1,)),
        dma((NX * NC - 1,)), dma((NX * NC - 1,)),
    ]
    return pl.pallas_call(
        kernel,
        out_shape=(
            jax.ShapeDtypeStruct((TOK, WIDTH), BF16),
            jax.ShapeDtypeStruct((1, D, WIDTH), BF16),
            jax.ShapeDtypeStruct((ROWS, WIDTH), F32),
        ),
        in_specs=[vmem, vmem, vmem, vmem, hbm],
        out_specs=(vmem, hbm, vmem),
        scratch_shapes=scratch,
        compiler_params=pltpu.CompilerParams(
            collective_id=0, has_side_effects=True, vmem_limit_bytes=48 * 1024 * 1024
        ),
    )(acts, grads_out, weight, basis_init, feedback)


def solution(mesh):
    return jax.shard_map(
        local,
        mesh=mesh,
        in_specs=(
            P("dp", "tensor"),
            P("dp", "tensor"),
            P("dp", "tensor"),
            P(None, "tensor"),
            P("dp", None, "tensor"),
        ),
        out_specs=(P("dp", "tensor"), P("dp", None, "tensor"), P("dp", "tensor")),
        check_vma=False,
    )
```

```python
import jax
import jax.numpy as jnp
from jax import lax
from jax.experimental import pallas as pl
from jax.experimental.pallas import tpu as pltpu
from jax.sharding import PartitionSpec as P

MESH = pl.DeviceIdType.MESH
F32 = jnp.float32
BF16 = jnp.bfloat16
RANK = 64
TOK = 128
WIDTH = 384
NT = 8
NX, NZ, NC = 4, 8, 2
ROWS = 48
D = NT * WIDTH

NN = (((1,), (0,)), ((), ()))
NTD = (((1,), (1,)), ((), ()))
TN = (((0,), (0,)), ((), ()))


def mm(a, b, dims):
    return lax.dot_general(a, b, dims, preferred_element_type=F32)


def mm32(a, b, dims):
    return lax.dot_general(
        a, b, dims, precision=lax.Precision.HIGHEST, preferred_element_type=F32
    )


def pieces(value, n):
    parts = []
    for _ in range(n):
        top = value.astype(BF16)
        parts.append(top)
        value = value - top.astype(F32)
    return jnp.concatenate(parts, axis=0)


def folded(stack, n):
    rows = stack.shape[0] // n
    total = stack[(n - 1) * rows :]
    for i in range(n - 2, -1, -1):
        total = total + stack[i * rows : (i + 1) * rows]
    return total


def eliminate(a, first, last):
    rows = lax.broadcasted_iota(jnp.int32, (RANK, 1), 0)
    for j in range(first, last):
        scaled = a[j : j + 1, :] / a[j : j + 1, j : j + 1]
        column = jnp.where(rows > j, a[:, j : j + 1], 0.0)
        a = a - column * scaled
    return a


def kernel(
    acts_hbm, grads_hbm, weight_hbm, basis_hbm, fb_hbm,
    ig_out, t0, ft, coefs,
    grads, weight, basis, fb, acts_all, grads_all, wbuf, fp, rc, f1, rx, f2, rz, f_all,
    sp, rs, rsz, sfull,
    in_sem,
    ring_s, ring_r, gr_s, gr_r, spread_s, spread_r, wz_s, wz_r, wx_s, wx_r, wy_s, wy_r, wc_s, wc_r,
    fc_s, fc_r, fx_s, fx_r, fz_s, fz_r, az_s, az_r, ax_s, ax_r, ac_s, ac_r,
    sx_s, sx_r, sz_s, sz_r, sa_s, sa_r,
):
    dp = lax.axis_index("dp")
    y = lax.axis_index("tensor")
    c = dp % NC
    z = (dp // NC) % NZ
    x = dp // (NC * NZ)

    def at(x_, z_, c_):
        return (x_ * NZ + z_) * NC + c_

    q = c * NX + x
    group = dp // NT
    pair_dp = y * NT + dp % NT
    y_peers = [(dp, (y + k) % NT) for k in range(1, NT)]
    z_peers = [(at(x, (z + k) % NZ, c), y) for k in range(1, NZ)]
    xc_peers = [
        (at((x + (o % NX)) % NX, z, (c + o // NX) % NC), y) for o in range(1, NX * NC)
    ]
    partner = xc_peers[NX - 1]
    x_peers = xc_peers[: NX - 1]
    swaps = group != y

    sends = []

    def send(src, dst, ssem, rsem, peer):
        cp = pltpu.make_async_remote_copy(
            src_ref=src, dst_ref=dst, send_sem=ssem, recv_sem=rsem,
            device_id=peer, device_id_type=MESH,
        )
        cp.start()
        sends.append(cp)
        return cp

    barrier = pltpu.get_barrier_semaphore()
    for peer in y_peers + z_peers + xc_peers:
        pl.semaphore_signal(barrier, inc=1, device_id=peer, device_id_type=MESH)

    @pl.when(swaps)
    def _():
        pl.semaphore_signal(barrier, inc=1, device_id=(pair_dp, group), device_id_type=MESH)

    loads = [
        pltpu.make_async_copy(src, dst, in_sem.at[i])
        for i, (src, dst) in enumerate([
            (acts_hbm, acts_all.at[y]), (weight_hbm, weight), (grads_hbm, grads),
            (basis_hbm, basis),
        ] + [
            (fb_hbm.at[0, pl.ds(t * WIDTH, WIDTH)], fb.at[t]) for t in range(NT)
        ])
    ]
    for cp in loads:
        cp.start()
    loads[0].wait()
    loads[1].wait()
    pl.semaphore_wait(barrier, 21 + jnp.where(swaps, 1, 0))

    bh, bc = (dp % NT) // NC, c
    mine = wbuf.at[group, bh, bc]
    swap = pltpu.make_async_remote_copy(
        src_ref=weight, dst_ref=wbuf.at[y, bh, bc], send_sem=spread_s, recv_sem=spread_r,
        device_id=(pair_dp, group), device_id_type=MESH,
    )

    @pl.when(swaps)
    def _():
        swap.start()

    @pl.when(jnp.logical_not(swaps))
    def _():
        wbuf[group, bh, bc] = weight[...]

    right = (dp, (y + 1) % NT)
    left = (dp, (y + NT - 1) % NT)
    quarter = TOK // 4

    def block_of(k, way):
        return (y - k + NT) % NT if way == 0 else (y + k) % NT

    def ring(way, k, h, peer):
        part = acts_all.at[block_of(k, way), pl.ds(h * quarter, quarter)]
        return send(part, part, ring_s.at[way, k, h], ring_r.at[way, k, h], peer)

    hops = {}
    for h in range(4):
        hops[0, 0, h] = ring(0, 0, h, right)
        hops[1, 0, h] = ring(1, 0, h, left)

    loads[2].wait()
    loads[3].wait()
    grads_all[y] = grads[...]
    bs = pieces(basis[...], 3)
    hs = pieces(folded(mm(bs, grads[...], NTD), 3), 3)

    core_cp, x_cp = {}, {}

    def add_acts(k, way):
        t = block_of(k, way)
        fp[t] = fp[t] + folded(mm(hs, acts_all[t], NN), 3)
        core_cp[k, way] = send(
            fp.at[t, pl.ds(32 * (1 - c), 32)], rc.at[t], fc_s.at[t], fc_r.at[t], partner
        )

    def x_stage(k, way):
        t = block_of(k, way)
        core_cp[k, way].wait_recv()
        f1[t] = fp[t, pl.ds(pl.multiple_of(32 * c, 32), 32)] + rc[t]
        for d in range(1, NX):
            to = (x + d) % NX
            x_cp[k, way, d] = send(
                f1.at[t, pl.ds(pl.multiple_of(8 * to, 8), 8)], rx.at[d - 1, t],
                fx_s.at[d - 1, t], fx_r.at[d - 1, t], x_peers[d - 1],
            )

    own = pl.ds(pl.multiple_of(8 * x, 8), 8)

    def z_stage(k, way):
        t = block_of(k, way)
        for d in range(1, NX):
            x_cp[k, way, d].wait_recv()
        f2[t] = f1[t, own] + rx[0, t] + rx[1, t] + rx[2, t]
        away = (t - z + NZ) % NZ

        @pl.when(away != 0)
        def _():
            z_copy(t, away).start()

    def z_copy(t, away):
        return pltpu.make_async_remote_copy(
            src_ref=f2.at[t], dst_ref=rz.at[away - 1], send_sem=fz_s.at[away - 1],
            recv_sem=fz_r.at[away - 1], device_id=(at(x, t, c), y), device_id_type=MESH,
        )

    ways = {0: [0], 1: [0, 1], 2: [0, 1], 3: [0, 1], 4: [0]}
    for k in range(5):
        if k:
            for h in range(4):
                for way, peer in ((0, right), (1, left)):
                    if (way, k - 1, h) in hops:
                        hops[way, k - 1, h].wait_recv()
                        if k < 3 or (k == 3 and h // 2 == way):
                            hops[way, k, h] = ring(way, k, h, peer)
        if k == 0:
            continue
        if k == 1:
            for cp in loads[4:]:
                cp.wait()
            for t in range(NT):
                fp[t] = folded(mm(bs, fb[t], NTD), 3)
            add_acts(0, 0)
        for way in ways[k]:
            add_acts(k, way)
        if k == 2:
            @pl.when(swaps)
            def _():
                swap.wait()
            wz = [
                send(mine, mine, wz_s.at[i], wz_r.at[i], z_peers[i]) for i in range(NZ - 1)
            ]
        if k >= 1:
            for way in ways[k - 1]:
                x_stage(k - 1, way)
        if k >= 3:
            for way in ways[k - 3]:
                z_stage(k - 3, way)

    gcp = [
        send(grads, grads_all.at[y], gr_s.at[i], gr_r.at[i], y_peers[i])
        for i in range(NT - 1)
    ]
    x_stage(4, 0)
    for k in (2, 3):
        for way in ways[k]:
            z_stage(k, way)
    for t in range(NT):
        t0[t] = mm(acts_all[t], grads[...], TN) + fb[t].astype(F32)
    z_stage(4, 0)
    for cp in wz:
        cp.wait_recv()
    wmine = wbuf.at[pl.ds(2 * x, 2), :, c]
    wx = {
        way: send(wmine, wmine, wx_s.at[way], wx_r.at[way], x_peers[(0, NX - 2)[way]])
        for way in (0, 1)
    }
    f3 = f2[z]
    zsum = [z_copy((z + i) % NZ, i) for i in range(1, NZ)]
    for i in range(NZ - 1):
        zsum[i].wait_recv()
        f3 = f3 + rz[i]

    top = f3.astype(BF16).astype(F32)
    f_all[z, q] = jnp.concatenate([top, f3 - top], axis=0).astype(BF16)
    az = [
        send(f_all.at[z, q], f_all.at[z, q], az_s.at[i], az_r.at[i], z_peers[i])
        for i in range(NZ - 1)
    ]
    ax, ac = {}, {}
    order = [0, 1, 7, 2, 6, 3, 5, 4]
    for o in order:
        zb = (z - o + NZ) % NZ
        if o:
            az[o - 1].wait_recv()
        for i in range(NX - 1):
            ax[o, i] = send(
                f_all.at[zb, q], f_all.at[zb, q], ax_s.at[i, zb], ax_r.at[i, zb], x_peers[i]
            )

    def unpaired(pairs):
        v = pairs.reshape(RANK // 8, 2, 8, pairs.shape[1])
        return (v[:, 0] + v[:, 1]).reshape(RANK, pairs.shape[1])

    through = jnp.zeros((2 * RANK, TOK), F32)
    direct = jnp.zeros((2 * RANK, WIDTH), F32)
    for o in order:
        zb = (z - o + NZ) % NZ
        for i in range(NX - 1):
            ax[o, i].wait_recv()
        part = f_all.at[zb, pl.ds(NX * c, NX)]
        ac[o] = send(part, part, ac_s.at[zb], ac_r.at[zb], partner)
    for some in (order[:4], order[4:]):
        for o in some:
            ac[o].wait_recv()
        for o in some:
            zb = (z - o + NZ) % NZ
            block = f_all[zb].reshape(2 * RANK, WIDTH)
            through = through + mm(block, acts_all[zb], NTD)
            direct = direct + mm(block, fb[zb], NN)
    local = unpaired(direct) + folded(mm(pieces(unpaired(through), 3), grads[...], NN), 3)
    sp[...] = local.reshape(RANK // 8, 8, WIDTH)
    sx = []
    for o in range(1, NX * NC):
        to = ((c + o // NX) % NC) * NX + (x + o % NX) % NX
        sx.append(
            send(sp.at[to], rs.at[o - 1], sx_s.at[o - 1], sx_r.at[o - 1], xc_peers[o - 1])
        )

    wy = {}
    for way in (0, 1):
        wx[way].wait_recv()
        part = wbuf.at[2 * ((x + (3, 1)[way]) % NX) + way, :, c]
        wy[way] = send(part, part, wy_s.at[way], wy_r.at[way], x_peers[(0, NX - 2)[way]])
    gram = jnp.zeros((2 * RANK, 2 * RANK), F32)
    for t in range(NT):
        block = f_all[t].reshape(2 * RANK, WIDTH)
        gram = gram + mm(block, block, NTD)
    lanes = lax.broadcasted_iota(jnp.int32, (2 * RANK, RANK), 0)
    cols = lax.broadcasted_iota(jnp.int32, (2 * RANK, RANK), 1)
    pick = jnp.where((lanes // 16) * 8 + lanes % 8 == cols, 1.0, 0.0)
    gram = mm32(unpaired(gram), pick, NN)
    eye = jnp.where(
        lax.broadcasted_iota(jnp.int32, (RANK, RANK), 0)
        == lax.broadcasted_iota(jnp.int32, (RANK, RANK), 1), 1.0, 0.0,
    )
    a = jnp.concatenate([gram, eye], axis=1)
    a = eliminate(a, 0, 12)

    s1 = sp[q]
    for i in range(NX * NC - 1):
        sx[i].wait_recv()
        s1 = s1 + rs[i]
    rsz[z] = s1
    sz = [
        send(rsz.at[z], rsz.at[z], sz_s.at[i], sz_r.at[i], z_peers[i]) for i in range(NZ - 1)
    ]
    a = eliminate(a, 12, 44)
    for cp in sz:
        cp.wait_recv()
    for way in (0, 1):
        wy[way].wait_recv()
    whalf = wbuf.at[:, :, c]
    wc = send(whalf, whalf, wc_s, wc_r, partner)
    s2 = rsz[0]
    for i in range(1, NZ):
        s2 = s2 + rsz[i]
    sfull[q] = s2
    sa = [
        send(sfull.at[q], sfull.at[q], sa_s.at[i], sa_r.at[i], xc_peers[i])
        for i in range(NX * NC - 1)
    ]
    a = eliminate(a, 44, RANK)
    for t in range(NT):
        ft[t] = (
            f_all[t].reshape(2 * RANK, WIDTH).astype(F32).T.astype(BF16)
        )
    pivots = jnp.sum(a[:, :RANK] * eye, axis=1, keepdims=True)
    inverse = a[:, RANK:]
    for cp in gcp:
        cp.wait_recv()
    wc.wait_recv()
    out = jnp.zeros((TOK, WIDTH), F32)
    for j in range(NT):
        out = out + mm(grads_all[j], wbuf[j].reshape(WIDTH, WIDTH), NTD)
    ig_out[...] = out.astype(BF16)

    for cp in sa:
        cp.wait_recv()

    solved = mm32(inverse, sfull[...].reshape(RANK, WIDTH), NN) / (pivots * 64.0)
    coef = mm32(inverse, solved, TN)
    ctop = coef.astype(BF16).astype(F32)

    def doubled(v):
        v = v.reshape(RANK // 8, 1, 8, WIDTH)
        return jnp.concatenate([v, v], axis=1).reshape(2 * RANK, WIDTH).astype(BF16)

    coefs[0], coefs[1] = doubled(ctop), doubled(coef - ctop)

    for cp in sends:
        cp.wait_send()
    for cp in zsum:
        cp.wait_send()


def finish(t0, ft, coefs, ig, ig_out, nf_out, up_out, nf, up, sems):
    def low_rank(left_side):
        return mm(left_side, coefs[0], NN) + mm(left_side, coefs[1], NN)

    stores = [pltpu.make_async_copy(ig, ig_out, sems.at[NT])]
    stores[0].start()
    dp = lax.axis_index("dp")
    first = pl.multiple_of((dp % NT) * ROWS, 16)
    up[...] = low_rank(ft[dp // NT, pl.ds(first, ROWS)])
    stores.append(pltpu.make_async_copy(up, up_out, sems.at[NT + 1]))
    stores[1].start()
    for t in range(NT):
        nf[t] = (t0[t] - low_rank(ft[t])).astype(BF16)
        stores.append(
            pltpu.make_async_copy(nf.at[t], nf_out.at[0, pl.ds(t * WIDTH, WIDTH)], sems.at[t])
        )
        stores[-1].start()
    for cp in stores:
        cp.wait()


def local(acts, grads_out, weight, basis_init, feedback):
    vmem = pl.BlockSpec(memory_space=pltpu.VMEM)
    hbm = pl.BlockSpec(memory_space=pltpu.HBM)
    dma = pltpu.SemaphoreType.DMA
    scratch = [
        pltpu.VMEM((TOK, WIDTH), BF16),
        pltpu.VMEM((ROWS, WIDTH), BF16),
        pltpu.VMEM((RANK, WIDTH), F32),
        pltpu.VMEM((NT, WIDTH, WIDTH), BF16),
        pltpu.VMEM((NT, TOK, WIDTH), BF16),
        pltpu.VMEM((NT, TOK, WIDTH), BF16),
        pltpu.VMEM((NT, 4, NC, ROWS, WIDTH), BF16),
        pltpu.VMEM((NT, RANK, WIDTH), F32),
        pltpu.VMEM((NT, RANK // 2, WIDTH), F32),
        pltpu.VMEM((NT, RANK // 2, WIDTH), F32),
        pltpu.VMEM((NX - 1, NT, 8, WIDTH), F32),
        pltpu.VMEM((NT, 8, WIDTH), F32),
        pltpu.VMEM((NZ - 1, 8, WIDTH), F32),
        pltpu.VMEM((NT, NX * NC, 16, WIDTH), BF16),
        pltpu.VMEM((NX * NC, 8, WIDTH), F32),
        pltpu.VMEM((NX * NC - 1, 8, WIDTH), F32),
        pltpu.VMEM((NZ, 8, WIDTH), F32),
        pltpu.VMEM((NX * NC, 8, WIDTH), F32),
        dma((4 + NT,)),
        dma((2, 4, 4)), dma((2, 4, 4)),
        dma((NT - 1,)), dma((NT - 1,)),
        dma, dma,
        dma((NZ - 1,)), dma((NZ - 1,)),
        dma((2,)), dma((2,)),
        dma((2,)), dma((2,)),
        dma, dma,
        dma((NT,)), dma((NT,)),
        dma((NX - 1, NT)), dma((NX - 1, NT)),
        dma((NZ - 1,)), dma((NZ - 1,)),
        dma((NZ - 1,)), dma((NZ - 1,)),
        dma((NX - 1, NZ)), dma((NX - 1, NZ)),
        dma((NZ,)), dma((NZ,)),
        dma((NX * NC - 1,)), dma((NX * NC - 1,)),
        dma((NZ - 1,)), dma((NZ - 1,)),
        dma((NX * NC - 1,)), dma((NX * NC - 1,)),
    ]
    parts = pl.pallas_call(
        kernel,
        out_shape=(
            jax.ShapeDtypeStruct((TOK, WIDTH), BF16),
            jax.ShapeDtypeStruct((NT, WIDTH, WIDTH), F32),
            jax.ShapeDtypeStruct((NT, WIDTH, 2 * RANK), BF16),
            jax.ShapeDtypeStruct((2, 2 * RANK, WIDTH), BF16),
        ),
        in_specs=[hbm] * 5,
        out_specs=(vmem,) * 4,
        scratch_shapes=scratch,
        compiler_params=pltpu.CompilerParams(
            collective_id=0, has_side_effects=True, vmem_limit_bytes=32 * 1024 * 1024
        ),
    )(*(
        pltpu.with_memory_space_constraint(v, pltpu.HBM)
        for v in (acts, grads_out, weight, basis_init, feedback)
    ))
    input_grads, total, factor_t, coefs = parts
    return pl.pallas_call(
        finish,
        out_shape=(
            jax.ShapeDtypeStruct((TOK, WIDTH), BF16),
            jax.ShapeDtypeStruct((1, D, WIDTH), BF16),
            jax.ShapeDtypeStruct((ROWS, WIDTH), F32),
        ),
        in_specs=[vmem] * 4,
        out_specs=(hbm,) * 3,
        scratch_shapes=[
            pltpu.VMEM((NT, WIDTH, WIDTH), BF16),
            pltpu.VMEM((ROWS, WIDTH), F32),
            dma((NT + 2,)),
        ],
        compiler_params=pltpu.CompilerParams(vmem_limit_bytes=20 * 1024 * 1024),
    )(total, factor_t, coefs, input_grads)


def solution(mesh):
    return jax.shard_map(
        local,
        mesh=mesh,
        in_specs=(
            P("dp", "tensor"),
            P("dp", "tensor"),
            P("dp", "tensor"),
            P(None, "tensor"),
            P("dp", None, "tensor"),
        ),
        out_specs=(P("dp", "tensor"), P("dp", None, "tensor"), P("dp", "tensor")),
        check_vma=False,
    )
```

```python
import jax
import jax.numpy as jnp
from jax import lax
from jax.experimental import pallas as pl
from jax.experimental.pallas import tpu as pltpu
from jax.sharding import PartitionSpec as P

MESH = pl.DeviceIdType.MESH
F32 = jnp.float32
BF16 = jnp.bfloat16
RANK = 64
TOK = 128
WIDTH = 384
NT = 8
NX, NZ, NC = 4, 8, 2
ROWS = 48
D = NT * WIDTH

NN = (((1,), (0,)), ((), ()))
NTD = (((1,), (1,)), ((), ()))
TN = (((0,), (0,)), ((), ()))


def mm(a, b, dims):
    return lax.dot_general(a, b, dims, preferred_element_type=F32)


def mm32(a, b, dims):
    return lax.dot_general(
        a, b, dims, precision=lax.Precision.HIGHEST, preferred_element_type=F32
    )


def pieces(value, n):
    parts = []
    for _ in range(n):
        top = value.astype(BF16)
        parts.append(top)
        value = value - top.astype(F32)
    return jnp.concatenate(parts, axis=0)


def folded(stack, n):
    rows = stack.shape[0] // n
    total = stack[(n - 1) * rows :]
    for i in range(n - 2, -1, -1):
        total = total + stack[i * rows : (i + 1) * rows]
    return total


def eliminate(a, first, last):
    rows = lax.broadcasted_iota(jnp.int32, (RANK, 1), 0)
    for j in range(first, last):
        scaled = a[j : j + 1, :] / a[j : j + 1, j : j + 1]
        column = jnp.where(rows > j, a[:, j : j + 1], 0.0)
        a = a - column * scaled
    return a


def kernel(
    acts_hbm, grads_hbm, weight_hbm, basis_hbm, fb_hbm,
    ig_out, t0, ft, coefs,
    grads, weight, basis, fb, acts_all, grads_all, wbuf, fp, rc, f1, rx, f2, rz, f_all,
    sp, rs, rsz, sfull,
    in_sem,
    sent, ring_r, gr_r, spread, wz_r, wx_r, wy_r, wc_r,
    fc_r, fx_r, fz_r, az_r, ax_r, ac_r, sx_r, sz_r, sa_r,
):
    dp = lax.axis_index("dp")
    y = lax.axis_index("tensor")
    c = dp % NC
    z = (dp // NC) % NZ
    x = dp // (NC * NZ)

    def at(x_, z_, c_):
        return (x_ * NZ + z_) * NC + c_

    q = c * NX + x
    group = dp // NT
    pair_dp = y * NT + dp % NT
    y_peers = [(dp, (y + k) % NT) for k in range(1, NT)]
    z_peers = [(at(x, (z + k) % NZ, c), y) for k in range(1, NZ)]
    xc_peers = [
        (at((x + (o % NX)) % NX, z, (c + o // NX) % NC), y) for o in range(1, NX * NC)
    ]
    partner = xc_peers[NX - 1]
    x_peers = xc_peers[: NX - 1]
    swaps = group != y

    sends = []

    def arrived(ref, rsem):
        pltpu.make_async_copy(ref, ref, rsem).wait()

    def send(src, dst, rsem, peer):
        cp = pltpu.make_async_remote_copy(
            src_ref=src, dst_ref=dst, send_sem=sent, recv_sem=rsem,
            device_id=peer, device_id_type=MESH,
        )
        cp.start()
        sends.append(cp)
        return cp

    barrier = pltpu.get_barrier_semaphore()
    for peer in y_peers + z_peers + xc_peers:
        pl.semaphore_signal(barrier, inc=1, device_id=peer, device_id_type=MESH)

    @pl.when(swaps)
    def _():
        pl.semaphore_signal(barrier, inc=1, device_id=(pair_dp, group), device_id_type=MESH)

    loads = [
        pltpu.make_async_copy(src, dst, in_sem.at[i])
        for i, (src, dst) in enumerate([
            (acts_hbm, acts_all.at[y]), (weight_hbm, weight), (grads_hbm, grads),
            (basis_hbm, basis),
            (fb_hbm.at[0], fb),
        ])
    ]
    for cp in loads:
        cp.start()
    loads[2].wait()
    loads[3].wait()
    grads_all[y] = grads[...]
    bs = pieces(basis[...], 3)
    hs = pieces(folded(mm(bs, grads[...], NTD), 3), 3)
    loads[4].wait()
    for t in range(NT):
        fp[t] = folded(mm(bs, fb[t * WIDTH : (t + 1) * WIDTH], NTD), 3)
    loads[0].wait()
    loads[1].wait()
    pl.semaphore_wait(barrier, 21 + jnp.where(swaps, 1, 0))

    bh, bc = (dp % NT) // NC, c
    mine = wbuf.at[group, bh, bc]
    swap = pltpu.make_async_remote_copy(
        src_ref=weight, dst_ref=wbuf.at[y, bh, bc], send_sem=spread.at[0], recv_sem=spread.at[1],
        device_id=(pair_dp, group), device_id_type=MESH,
    )

    @pl.when(swaps)
    def _():
        swap.start()

    @pl.when(jnp.logical_not(swaps))
    def _():
        wbuf[group, bh, bc] = weight[...]

    right = (dp, (y + 1) % NT)
    left = (dp, (y + NT - 1) % NT)
    quarter = TOK // 4

    def block_of(k, way):
        return (y - k + NT) % NT if way == 0 else (y + k) % NT

    def ring(way, k, h, peer):
        part = acts_all.at[block_of(k, way), pl.ds(h * quarter, quarter)]
        return send(part, part, ring_r.at[way, k, h], peer)

    hops = {}
    for h in range(4):
        hops[0, 0, h] = ring(0, 0, h, right)
        hops[1, 0, h] = ring(1, 0, h, left)

    core_cp = {}

    def add_acts(k, way):
        t = block_of(k, way)
        fp[t] = fp[t] + folded(mm(hs, acts_all[t], NN), 3)
        core_cp[k, way] = send(
            fp.at[t, pl.ds(32 * (1 - c), 32)], rc.at[t], fc_r.at[t], partner
        )

    def x_stage(k, way):
        t = block_of(k, way)
        core_cp[k, way].wait_recv()
        f1[t] = fp[t, pl.ds(pl.multiple_of(32 * c, 32), 32)] + rc[t]
        for d in range(1, NX):
            to = (x + d) % NX
            send(
                f1.at[t, pl.ds(pl.multiple_of(8 * to, 8), 8)], rx.at[t, d - 1],
                fx_r.at[t], x_peers[d - 1],
            )

    own = pl.ds(pl.multiple_of(8 * x, 8), 8)

    def z_stage(k, way):
        t = block_of(k, way)
        arrived(rx.at[t], fx_r.at[t])
        f2[t] = f1[t, own] + rx[t, 0] + rx[t, 1] + rx[t, 2]
        away = (t - z + NZ) % NZ

        @pl.when(away != 0)
        def _():
            z_copy(t, away).start()

    def z_copy(t, away):
        return pltpu.make_async_remote_copy(
            src_ref=f2.at[t], dst_ref=rz.at[away - 1], send_sem=sent,
            recv_sem=fz_r, device_id=(at(x, t, c), y), device_id_type=MESH,
        )

    ways = {0: [0], 1: [0, 1], 2: [0, 1], 3: [0, 1], 4: [0]}
    for k in range(5):
        if k:
            for h in range(4):
                for way, peer in ((0, right), (1, left)):
                    if (way, k - 1, h) in hops:
                        hops[way, k - 1, h].wait_recv()
                        if k < 3 or (k == 3 and h // 2 == way):
                            hops[way, k, h] = ring(way, k, h, peer)
        if k >= 1:
            for way in ways[k - 1]:
                x_stage(k - 1, way)
        for way in ways[k]:
            add_acts(k, way)
        if k == 2:
            @pl.when(swaps)
            def _():
                swap.wait_recv()
            for i in range(NZ - 1):
                send(mine, mine, wz_r, z_peers[i])
        if k >= 3:
            for way in ways[k - 3]:
                z_stage(k - 3, way)

    for i in range(NT - 1):
        send(grads, grads_all.at[y], gr_r, y_peers[i])
    x_stage(4, 0)
    for t in range(NT):
        t0[t] = mm(acts_all[t], grads[...], TN) + fb[t * WIDTH : (t + 1) * WIDTH].astype(F32)
    for k in (2, 3):
        for way in ways[k]:
            z_stage(k, way)
    z_stage(4, 0)
    arrived(wbuf.at[0:NZ - 1, 0, 0], wz_r)
    piece = wbuf.at[pl.ds(2 * x, 2), :, c]
    wx = [
        send(piece, piece, wx_r.at[way], x_peers[(0, NX - 2)[way]]) for way in (0, 1)
    ]
    f3 = f2[z]
    zsum = [z_copy((z + i) % NZ, i) for i in range(1, NZ)]
    arrived(rz, fz_r)
    for i in range(NZ - 1):
        f3 = f3 + rz[i]

    top = f3.astype(BF16).astype(F32)
    f_all[z, q] = jnp.concatenate([top, f3 - top], axis=0).astype(BF16)
    az = [
        send(f_all.at[z, q], f_all.at[z, q], az_r.at[i], z_peers[i])
        for i in range(NZ - 1)
    ]
    ac = {}
    order = [0, 1, 7, 2, 6, 3, 5, 4]
    for o in order:
        zb = (z - o + NZ) % NZ
        if o:
            az[o - 1].wait_recv()
        for i in range(NX - 1):
            send(f_all.at[zb, q], f_all.at[zb, q], ax_r.at[zb], x_peers[i])

    def unpaired(pairs):
        v = pairs.reshape(RANK // 8, 2, 8, pairs.shape[1])
        return (v[:, 0] + v[:, 1]).reshape(RANK, pairs.shape[1])

    through = jnp.zeros((2 * RANK, TOK), F32)
    direct = jnp.zeros((2 * RANK, WIDTH), F32)
    for o in order:
        zb = (z - o + NZ) % NZ
        arrived(f_all.at[zb, pl.ds(0, NX - 1)], ax_r.at[zb])
        part = f_all.at[zb, pl.ds(NX * c, NX)]
        ac[o] = send(part, part, ac_r.at[zb], partner)
    for some in (order[:4], order[4:]):
        for o in some:
            ac[o].wait_recv()
        for o in some:
            zb = (z - o + NZ) % NZ
            block = f_all[zb].reshape(2 * RANK, WIDTH)
            through = through + mm(block, acts_all[zb], NTD)
            direct = direct + mm(block, fb[pl.ds(pl.multiple_of(zb * WIDTH, WIDTH), WIDTH)], NN)
    local = unpaired(direct) + folded(mm(pieces(unpaired(through), 3), grads[...], NN), 3)
    sp[...] = local.reshape(RANK // 8, 8, WIDTH)
    for o in range(1, NX * NC):
        to = ((c + o // NX) % NC) * NX + (x + o % NX) % NX
        send(sp.at[to], rs.at[o - 1], sx_r, xc_peers[o - 1])

    wy = []
    for way in (0, 1):
        wx[way].wait_recv()
        piece = wbuf.at[2 * ((x + (NX - 1, 1)[way]) % NX) + way, :, c]
        wy.append(send(piece, piece, wy_r.at[way], x_peers[(0, NX - 2)[way]]))
    gram = jnp.zeros((2 * RANK, 2 * RANK), F32)
    for t in range(NT):
        block = f_all[t].reshape(2 * RANK, WIDTH)
        gram = gram + mm(block, block, NTD)
    lanes = lax.broadcasted_iota(jnp.int32, (2 * RANK, RANK), 0)
    cols = lax.broadcasted_iota(jnp.int32, (2 * RANK, RANK), 1)
    pick = jnp.where((lanes // 16) * 8 + lanes % 8 == cols, 1.0, 0.0)
    gram = mm32(unpaired(gram), pick, NN)
    eye = jnp.where(
        lax.broadcasted_iota(jnp.int32, (RANK, RANK), 0)
        == lax.broadcasted_iota(jnp.int32, (RANK, RANK), 1), 1.0, 0.0,
    )
    a = jnp.concatenate([gram, eye], axis=1)
    a = eliminate(a, 0, 12)

    arrived(rs, sx_r)
    s1 = sp[q]
    for i in range(NX * NC - 1):
        s1 = s1 + rs[i]
    rsz[z] = s1
    for i in range(NZ - 1):
        send(rsz.at[z], rsz.at[z], sz_r, z_peers[i])
    a = eliminate(a, 12, 44)
    arrived(rsz.at[pl.ds(0, NZ - 1)], sz_r)
    for cp in wy:
        cp.wait_recv()
    whalf = wbuf.at[:, :, c]
    wc = send(whalf, whalf, wc_r, partner)
    s2 = rsz[0]
    for i in range(1, NZ):
        s2 = s2 + rsz[i]
    sfull[q] = s2
    for i in range(NX * NC - 1):
        send(sfull.at[q], sfull.at[q], sa_r, xc_peers[i])
    a = eliminate(a, 44, RANK)
    for t in range(NT):
        ft[t] = (
            f_all[t].reshape(2 * RANK, WIDTH).astype(F32).T.astype(BF16)
        )
    pivots = jnp.sum(a[:, :RANK] * eye, axis=1, keepdims=True)
    inverse = a[:, RANK:]
    arrived(grads_all.at[pl.ds(0, NT - 1)], gr_r)
    wc.wait_recv()
    out = jnp.zeros((TOK, WIDTH), F32)
    for j in range(NT):
        out = out + mm(grads_all[j], wbuf[j].reshape(WIDTH, WIDTH), NTD)
    ig_out[...] = out.astype(BF16)

    arrived(sfull.at[pl.ds(0, NX * NC - 1)], sa_r)

    solved = mm32(inverse, sfull[...].reshape(RANK, WIDTH), NN) / (pivots * 64.0)
    coef = mm32(inverse, solved, TN)
    ctop = coef.astype(BF16).astype(F32)

    def doubled(v):
        v = v.reshape(RANK // 8, 1, 8, WIDTH)
        return jnp.concatenate([v, v], axis=1).reshape(2 * RANK, WIDTH).astype(BF16)

    coefs[0], coefs[1] = doubled(ctop), doubled(coef - ctop)

    for cp in sends:
        cp.wait_send()
    for cp in zsum:
        cp.wait_send()

    @pl.when(swaps)
    def _():
        swap.wait_send()


def finish(t0, ft, coefs, ig, ig_out, nf_out, up_out, nf, up, sems):
    def low_rank(left_side):
        return mm(left_side, coefs[0], NN) + mm(left_side, coefs[1], NN)

    stores = [pltpu.make_async_copy(ig, ig_out, sems.at[NT])]
    stores[0].start()
    dp = lax.axis_index("dp")
    first = pl.multiple_of((dp % NT) * ROWS, 16)
    up[...] = low_rank(ft[dp // NT, pl.ds(first, ROWS)])
    stores.append(pltpu.make_async_copy(up, up_out, sems.at[NT + 1]))
    stores[1].start()
    for t in range(NT):
        nf[t] = (t0[t] - low_rank(ft[t])).astype(BF16)
        stores.append(
            pltpu.make_async_copy(nf.at[t], nf_out.at[0, pl.ds(t * WIDTH, WIDTH)], sems.at[t])
        )
        stores[-1].start()
    for cp in stores:
        cp.wait()


def local(acts, grads_out, weight, basis_init, feedback):
    vmem = pl.BlockSpec(memory_space=pltpu.VMEM)
    hbm = pl.BlockSpec(memory_space=pltpu.HBM)
    dma = pltpu.SemaphoreType.DMA
    scratch = [
        pltpu.VMEM((TOK, WIDTH), BF16),
        pltpu.VMEM((ROWS, WIDTH), BF16),
        pltpu.VMEM((RANK, WIDTH), F32),
        pltpu.VMEM((D, WIDTH), BF16),
        pltpu.VMEM((NT, TOK, WIDTH), BF16),
        pltpu.VMEM((NT, TOK, WIDTH), BF16),
        pltpu.VMEM((NT, 4, NC, ROWS, WIDTH), BF16),
        pltpu.VMEM((NT, RANK, WIDTH), F32),
        pltpu.VMEM((NT, RANK // 2, WIDTH), F32),
        pltpu.VMEM((NT, RANK // 2, WIDTH), F32),
        pltpu.VMEM((NT, NX - 1, 8, WIDTH), F32),
        pltpu.VMEM((NT, 8, WIDTH), F32),
        pltpu.VMEM((NZ - 1, 8, WIDTH), F32),
        pltpu.VMEM((NT, NX * NC, 16, WIDTH), BF16),
        pltpu.VMEM((NX * NC, 8, WIDTH), F32),
        pltpu.VMEM((NX * NC - 1, 8, WIDTH), F32),
        pltpu.VMEM((NZ, 8, WIDTH), F32),
        pltpu.VMEM((NX * NC, 8, WIDTH), F32),
        dma((5,)),
        dma,
        dma((2, 4, 4)),
        dma,
        dma((2,)),
        dma,
        dma((2,)),
        dma((2,)),
        dma,
        dma((NT,)),
        dma((NT,)),
        dma,
        dma((NZ - 1,)),
        dma((NZ,)),
        dma((NZ,)),
        dma,
        dma,
        dma,
    ]
    parts = pl.pallas_call(
        kernel,
        out_shape=(
            jax.ShapeDtypeStruct((TOK, WIDTH), BF16),
            jax.ShapeDtypeStruct((NT, WIDTH, WIDTH), F32),
            jax.ShapeDtypeStruct((NT, WIDTH, 2 * RANK), BF16),
            jax.ShapeDtypeStruct((2, 2 * RANK, WIDTH), BF16),
        ),
        in_specs=[hbm] * 5,
        out_specs=(vmem,) * 4,
        scratch_shapes=scratch,
        compiler_params=pltpu.CompilerParams(
            collective_id=0, has_side_effects=True, vmem_limit_bytes=32 * 1024 * 1024
        ),
    )(*(
        pltpu.with_memory_space_constraint(v, pltpu.HBM)
        for v in (acts, grads_out, weight, basis_init, feedback)
    ))
    input_grads, total, factor_t, coefs = parts
    return pl.pallas_call(
        finish,
        out_shape=(
            jax.ShapeDtypeStruct((TOK, WIDTH), BF16),
            jax.ShapeDtypeStruct((1, D, WIDTH), BF16),
            jax.ShapeDtypeStruct((ROWS, WIDTH), F32),
        ),
        in_specs=[vmem] * 4,
        out_specs=(hbm,) * 3,
        scratch_shapes=[
            pltpu.VMEM((NT, WIDTH, WIDTH), BF16),
            pltpu.VMEM((ROWS, WIDTH), F32),
            dma((NT + 2,)),
        ],
        compiler_params=pltpu.CompilerParams(vmem_limit_bytes=20 * 1024 * 1024),
    )(total, factor_t, coefs, input_grads)


def solution(mesh):
    return jax.shard_map(
        local,
        mesh=mesh,
        in_specs=(
            P("dp", "tensor"),
            P("dp", "tensor"),
            P("dp", "tensor"),
            P(None, "tensor"),
            P("dp", None, "tensor"),
        ),
        out_specs=(P("dp", "tensor"), P("dp", None, "tensor"), P("dp", "tensor")),
        check_vma=False,
    )
```

```python
import jax
import jax.numpy as jnp
from jax import lax
from jax.experimental import pallas as pl
from jax.experimental.pallas import tpu as pltpu
from jax.sharding import PartitionSpec as P

MESH = pl.DeviceIdType.MESH
F32 = jnp.float32
BF16 = jnp.bfloat16
RANK = 64
TOK = 128
WIDTH = 384
NT = 8
NX, NZ, NC = 4, 8, 2
ROWS = 48
D = NT * WIDTH

NN = (((1,), (0,)), ((), ()))
NTD = (((1,), (1,)), ((), ()))
TN = (((0,), (0,)), ((), ()))


def mm(a, b, dims):
    return lax.dot_general(a, b, dims, preferred_element_type=F32)


def mm32(a, b, dims):
    return lax.dot_general(
        a, b, dims, precision=lax.Precision.HIGHEST, preferred_element_type=F32
    )


def pieces(value, n):
    parts = []
    for _ in range(n):
        top = value.astype(BF16)
        parts.append(top)
        value = value - top.astype(F32)
    return jnp.concatenate(parts, axis=0)


def folded(stack, n):
    rows = stack.shape[0] // n
    total = stack[(n - 1) * rows :]
    for i in range(n - 2, -1, -1):
        total = total + stack[i * rows : (i + 1) * rows]
    return total


def eliminate(a, first, last):
    rows = lax.broadcasted_iota(jnp.int32, (RANK, 1), 0)
    for j in range(first, last):
        scaled = a[j : j + 1, :] / a[j : j + 1, j : j + 1]
        column = jnp.where(rows > j, a[:, j : j + 1], 0.0)
        a = a - column * scaled
    return a


def kernel(
    acts_hbm, grads_hbm, weight_hbm, basis_hbm, fb_hbm,
    ig_out, t0, ft, coefs,
    grads, weight, basis, fb, acts_all, grads_all, wbuf, fp, rc, f1, rx, f2, rz, rzx, f_all,
    sp, rs, rsz, sfull,
    in_sem,
    sent, ring_r, gr_r, spread, wz_r, wx_r, wy_r, wc_r,
    fc_r, fx_r, fz_r, zx_r, az_r, ax_r, ac_r, sx_r, sz_r, sa_r,
):
    dp = lax.axis_index("dp")
    y = lax.axis_index("tensor")
    c = dp % NC
    z = (dp // NC) % NZ
    x = dp // (NC * NZ)

    def at(x_, z_, c_):
        return (x_ * NZ + z_) * NC + c_

    q = c * NX + x
    group = dp // NT
    pair_dp = y * NT + dp % NT
    y_peers = [(dp, (y + k) % NT) for k in range(1, NT)]
    z_peers = [(at(x, (z + k) % NZ, c), y) for k in range(1, NZ)]
    xc_peers = [
        (at((x + (o % NX)) % NX, z, (c + o // NX) % NC), y) for o in range(1, NX * NC)
    ]
    partner = xc_peers[NX - 1]
    x_peers = xc_peers[: NX - 1]
    swaps = group != y

    sends = []

    def arrived(ref, rsem):
        pltpu.make_async_copy(ref, ref, rsem).wait()

    def send(src, dst, rsem, peer):
        cp = pltpu.make_async_remote_copy(
            src_ref=src, dst_ref=dst, send_sem=sent, recv_sem=rsem,
            device_id=peer, device_id_type=MESH,
        )
        cp.start()
        sends.append(cp)
        return cp

    barrier = pltpu.get_barrier_semaphore()
    for peer in y_peers + z_peers + xc_peers:
        pl.semaphore_signal(barrier, inc=1, device_id=peer, device_id_type=MESH)

    @pl.when(swaps)
    def _():
        pl.semaphore_signal(barrier, inc=1, device_id=(pair_dp, group), device_id_type=MESH)

    loads = [
        pltpu.make_async_copy(src, dst, in_sem.at[i])
        for i, (src, dst) in enumerate([
            (acts_hbm, acts_all.at[y]), (weight_hbm, weight), (grads_hbm, grads),
            (basis_hbm, basis),
            (fb_hbm.at[0], fb),
        ])
    ]
    for cp in loads:
        cp.start()
    loads[2].wait()
    loads[3].wait()
    grads_all[y] = grads[...]
    bs = pieces(basis[...], 3)
    hs = pieces(folded(mm(bs, grads[...], NTD), 3), 3)
    loads[4].wait()
    for t in range(NT):
        fp[t] = folded(mm(bs, fb[t * WIDTH : (t + 1) * WIDTH], NTD), 3)
    loads[0].wait()
    loads[1].wait()
    pl.semaphore_wait(barrier, 21 + jnp.where(swaps, 1, 0))

    bh, bc = (dp % NT) // NC, c
    mine = wbuf.at[group, bh, bc]
    swap = pltpu.make_async_remote_copy(
        src_ref=weight, dst_ref=wbuf.at[y, bh, bc], send_sem=spread.at[0], recv_sem=spread.at[1],
        device_id=(pair_dp, group), device_id_type=MESH,
    )

    @pl.when(swaps)
    def _():
        swap.start()

    @pl.when(jnp.logical_not(swaps))
    def _():
        wbuf[group, bh, bc] = weight[...]

    right = (dp, (y + 1) % NT)
    left = (dp, (y + NT - 1) % NT)
    quarter = TOK // 4

    def block_of(k, way):
        return (y - k + NT) % NT if way == 0 else (y + k) % NT

    def ring(way, k, h, peer):
        part = acts_all.at[block_of(k, way), pl.ds(h * quarter, quarter)]
        return send(part, part, ring_r.at[way, k, h], peer)

    hops = {}
    for h in range(4):
        hops[0, 0, h] = ring(0, 0, h, right)
        hops[1, 0, h] = ring(1, 0, h, left)

    core_cp = {}

    def add_acts(k, way):
        t = block_of(k, way)
        fp[t] = fp[t] + folded(mm(hs, acts_all[t], NN), 3)
        core_cp[k, way] = send(
            fp.at[t, pl.ds(32 * (1 - c), 32)], rc.at[t], fc_r.at[t], partner
        )

    def x_stage(k, way):
        t = block_of(k, way)
        core_cp[k, way].wait_recv()
        f1[t] = fp[t, pl.ds(pl.multiple_of(32 * c, 32), 32)] + rc[t]
        for d in range(1, NX):
            to = (x + d) % NX
            send(
                f1.at[t, pl.ds(pl.multiple_of(8 * to, 8), 8)], rx.at[t, d - 1],
                fx_r.at[t], x_peers[d - 1],
            )

    own = pl.ds(pl.multiple_of(8 * x, 8), 8)

    def z_copy(t, away):
        return pltpu.make_async_remote_copy(
            src_ref=f2.at[t], dst_ref=rz.at[away - 1], send_sem=sent,
            recv_sem=fz_r, device_id=(at(x, t, c), y), device_id_type=MESH,
        )

    def back_copy(t, i):
        return pltpu.make_async_remote_copy(
            src_ref=f_all.at[t, q], dst_ref=f_all.at[t, q], send_sem=sent,
            recv_sem=az_r.at[t], device_id=z_peers[i], device_id_type=MESH,
        )

    def x_sum(t):
        arrived(rx.at[t], fx_r.at[t])
        return f1[t, own] + rx[t, 0] + rx[t, 1] + rx[t, 2]

    def z_stage(k, way):
        t = block_of(k, way)
        f2[t] = x_sum(t)
        away = (t - z + NZ) % NZ

        @pl.when(away != 0)
        def _():
            z_copy(t, away).start()

    def keep(t, f3):
        top = f3.astype(BF16).astype(F32)
        f_all[t, q] = jnp.concatenate([top, f3 - top], axis=0).astype(BF16)

    def owner_stage(k, way):
        t = block_of(k, way)

        @pl.when(t == z)
        def _():
            arrived(rz, fz_r)
            f3 = f2[t]
            for i in range(NZ - 1):
                f3 = f3 + rz[i]
            keep(t, f3)
            for i in range(NZ - 1):
                back_copy(t, i).start()

    def back_x_sends(t):
        for i in range(NX - 1):
            send(f_all.at[t, q], f_all.at[t, q], ax_r.at[t], x_peers[i])

    def back_x(k, way):
        t = block_of(k, way)

        @pl.when(t != z)
        def _():
            arrived(f_all.at[t, q], az_r.at[t])

        back_x_sends(t)

    def last_z_stage():
        rzx[z] = x_sum(block_of(4, 0))
        for i in range(NZ - 1):
            send(rzx.at[z], rzx.at[z], zx_r, z_peers[i])

    def last_back_x():
        arrived(rzx.at[pl.ds(0, NZ - 1)], zx_r)
        f3 = rzx[0]
        for i in range(1, NZ):
            f3 = f3 + rzx[i]
        keep(block_of(4, 0), f3)
        back_x_sends(block_of(4, 0))

    back_core = {}

    def back_core_stage(k, way):
        t = block_of(k, way)
        arrived(f_all.at[t, pl.ds(0, NX - 1)], ax_r.at[t])
        part = f_all.at[t, pl.ds(NX * c, NX)]
        back_core[k, way] = send(part, part, ac_r.at[t], partner)

    through = jnp.zeros((2 * RANK, TOK), F32)
    direct = jnp.zeros((2 * RANK, WIDTH), F32)

    def second_part(through, direct, which):
        for key in which:
            back_core[key].wait_recv()
        for key in which:
            t = block_of(*key)
            block = f_all[t].reshape(2 * RANK, WIDTH)
            rows = pl.ds(pl.multiple_of(t * WIDTH, WIDTH), WIDTH)
            through = through + mm(block, acts_all[t], NTD)
            direct = direct + mm(block, fb[rows], NN)
        return through, direct

    ways = {0: [0], 1: [0, 1], 2: [0, 1], 3: [0, 1], 4: [0]}

    def each(stage, k):
        for way in ways[k]:
            stage(k, way)

    for k in range(5):
        if k == 4:
            each(x_stage, 3)
            each(z_stage, 1)
        if k:
            for h in range(4):
                for way, peer in ((0, right), (1, left)):
                    if (way, k - 1, h) in hops:
                        hops[way, k - 1, h].wait_recv()
                        if k < 3 or (k == 3 and h // 2 == way):
                            hops[way, k, h] = ring(way, k, h, peer)
        each(add_acts, k)
        if 1 <= k < 4:
            each(x_stage, k - 1)
        if k == 2:
            @pl.when(swaps)
            def _():
                swap.wait_recv()
            for i in range(NZ - 1):
                send(mine, mine, wz_r, z_peers[i])
        if k == 3:
            each(z_stage, 0)

    each(x_stage, 4)
    for i in range(NT - 1):
        send(grads, grads_all.at[y], gr_r, y_peers[i])
    each(owner_stage, 0)
    each(z_stage, 2)
    for t in range(NT):
        t0[t] = mm(acts_all[t], grads[...], TN) + fb[t * WIDTH : (t + 1) * WIDTH].astype(F32)
    arrived(wbuf.at[0:NZ - 1, 0, 0], wz_r)
    piece = wbuf.at[pl.ds(2 * x, 2), :, c]
    wx = [
        send(piece, piece, wx_r.at[way], x_peers[(0, NX - 2)[way]]) for way in (0, 1)
    ]
    each(z_stage, 3)
    last_z_stage()
    each(owner_stage, 1)
    each(back_x, 0)
    each(owner_stage, 2)
    each(owner_stage, 3)
    each(back_x, 1)
    last_back_x()
    each(back_x, 2)
    each(back_core_stage, 0)
    each(back_core_stage, 1)
    each(back_x, 3)
    each(back_core_stage, 2)
    through, direct = second_part(through, direct, [(0, 0), (1, 0), (1, 1)])
    each(back_core_stage, 4)
    each(back_core_stage, 3)
    through, direct = second_part(through, direct, [(2, 0), (2, 1)])
    through, direct = second_part(through, direct, [(4, 0), (3, 0), (3, 1)])

    def unpaired(pairs):
        v = pairs.reshape(RANK // 8, 2, 8, pairs.shape[1])
        return (v[:, 0] + v[:, 1]).reshape(RANK, pairs.shape[1])

    local = unpaired(direct) + folded(mm(pieces(unpaired(through), 3), grads[...], NN), 3)
    sp[...] = local.reshape(RANK // 8, 8, WIDTH)
    for o in range(1, NX * NC):
        to = ((c + o // NX) % NC) * NX + (x + o % NX) % NX
        send(sp.at[to], rs.at[o - 1], sx_r, xc_peers[o - 1])

    wy = []
    for way in (0, 1):
        wx[way].wait_recv()
        piece = wbuf.at[2 * ((x + (NX - 1, 1)[way]) % NX) + way, :, c]
        wy.append(send(piece, piece, wy_r.at[way], x_peers[(0, NX - 2)[way]]))
    gram = jnp.zeros((2 * RANK, 2 * RANK), F32)
    for t in range(NT):
        block = f_all[t].reshape(2 * RANK, WIDTH)
        gram = gram + mm(block, block, NTD)
    lanes = lax.broadcasted_iota(jnp.int32, (2 * RANK, RANK), 0)
    cols = lax.broadcasted_iota(jnp.int32, (2 * RANK, RANK), 1)
    pick = jnp.where((lanes // 16) * 8 + lanes % 8 == cols, 1.0, 0.0)
    gram = mm32(unpaired(gram), pick, NN)
    eye = jnp.where(
        lax.broadcasted_iota(jnp.int32, (RANK, RANK), 0)
        == lax.broadcasted_iota(jnp.int32, (RANK, RANK), 1), 1.0, 0.0,
    )
    a = jnp.concatenate([gram, eye], axis=1)
    a = eliminate(a, 0, 12)

    arrived(rs, sx_r)
    s1 = sp[q]
    for i in range(NX * NC - 1):
        s1 = s1 + rs[i]
    rsz[z] = s1
    for i in range(NZ - 1):
        send(rsz.at[z], rsz.at[z], sz_r, z_peers[i])
    a = eliminate(a, 12, 44)
    arrived(rsz.at[pl.ds(0, NZ - 1)], sz_r)
    for cp in wy:
        cp.wait_recv()
    whalf = wbuf.at[:, :, c]
    wc = send(whalf, whalf, wc_r, partner)
    s2 = rsz[0]
    for i in range(1, NZ):
        s2 = s2 + rsz[i]
    sfull[q] = s2
    for i in range(NX * NC - 1):
        send(sfull.at[q], sfull.at[q], sa_r, xc_peers[i])
    a = eliminate(a, 44, RANK)
    for t in range(NT):
        ft[t] = (
            f_all[t].reshape(2 * RANK, WIDTH).astype(F32).T.astype(BF16)
        )
    pivots = jnp.sum(a[:, :RANK] * eye, axis=1, keepdims=True)
    inverse = a[:, RANK:]
    arrived(grads_all.at[pl.ds(0, NT - 1)], gr_r)
    wc.wait_recv()
    out = jnp.zeros((TOK, WIDTH), F32)
    for j in range(NT):
        out = out + mm(grads_all[j], wbuf[j].reshape(WIDTH, WIDTH), NTD)
    ig_out[...] = out.astype(BF16)

    arrived(sfull.at[pl.ds(0, NX * NC - 1)], sa_r)

    solved = mm32(inverse, sfull[...].reshape(RANK, WIDTH), NN) / (pivots * 64.0)
    coef = mm32(inverse, solved, TN)
    ctop = coef.astype(BF16).astype(F32)

    def doubled(v):
        v = v.reshape(RANK // 8, 1, 8, WIDTH)
        return jnp.concatenate([v, v], axis=1).reshape(2 * RANK, WIDTH).astype(BF16)

    coefs[0], coefs[1] = doubled(ctop), doubled(coef - ctop)

    for cp in sends:
        cp.wait_send()
    for t in [block_of(k, way) for k in range(4) for way in ways[k]]:
        @pl.when(t != z)
        def _():
            z_copy(t, (t - z + NZ) % NZ).wait_send()

        @pl.when(t == z)
        def _():
            for i in range(NZ - 1):
                back_copy(t, i).wait_send()

    @pl.when(swaps)
    def _():
        swap.wait_send()


def finish(t0, ft, coefs, ig, ig_out, nf_out, up_out, nf, up, sems):
    def low_rank(left_side):
        return mm(left_side, coefs[0], NN) + mm(left_side, coefs[1], NN)

    stores = [pltpu.make_async_copy(ig, ig_out, sems.at[NT])]
    stores[0].start()
    dp = lax.axis_index("dp")
    first = pl.multiple_of((dp % NT) * ROWS, 16)
    up[...] = low_rank(ft[dp // NT, pl.ds(first, ROWS)])
    stores.append(pltpu.make_async_copy(up, up_out, sems.at[NT + 1]))
    stores[1].start()
    for t in range(NT):
        nf[t] = (t0[t] - low_rank(ft[t])).astype(BF16)
        stores.append(
            pltpu.make_async_copy(nf.at[t], nf_out.at[0, pl.ds(t * WIDTH, WIDTH)], sems.at[t])
        )
        stores[-1].start()
    for cp in stores:
        cp.wait()


def local(acts, grads_out, weight, basis_init, feedback):
    vmem = pl.BlockSpec(memory_space=pltpu.VMEM)
    hbm = pl.BlockSpec(memory_space=pltpu.HBM)
    dma = pltpu.SemaphoreType.DMA
    scratch = [
        pltpu.VMEM((TOK, WIDTH), BF16),
        pltpu.VMEM((ROWS, WIDTH), BF16),
        pltpu.VMEM((RANK, WIDTH), F32),
        pltpu.VMEM((D, WIDTH), BF16),
        pltpu.VMEM((NT, TOK, WIDTH), BF16),
        pltpu.VMEM((NT, TOK, WIDTH), BF16),
        pltpu.VMEM((NT, 4, NC, ROWS, WIDTH), BF16),
        pltpu.VMEM((NT, RANK, WIDTH), F32),
        pltpu.VMEM((NT, RANK // 2, WIDTH), F32),
        pltpu.VMEM((NT, RANK // 2, WIDTH), F32),
        pltpu.VMEM((NT, NX - 1, 8, WIDTH), F32),
        pltpu.VMEM((NT, 8, WIDTH), F32),
        pltpu.VMEM((NZ - 1, 8, WIDTH), F32),
        pltpu.VMEM((NZ, 8, WIDTH), F32),
        pltpu.VMEM((NT, NX * NC, 16, WIDTH), BF16),
        pltpu.VMEM((NX * NC, 8, WIDTH), F32),
        pltpu.VMEM((NX * NC - 1, 8, WIDTH), F32),
        pltpu.VMEM((NZ, 8, WIDTH), F32),
        pltpu.VMEM((NX * NC, 8, WIDTH), F32),
        dma((5,)),
        dma,
        dma((2, 4, 4)),
        dma,
        dma((2,)),
        dma,
        dma((2,)),
        dma((2,)),
        dma,
        dma((NT,)),
        dma((NT,)),
        dma,
        dma,
        dma((NZ,)),
        dma((NZ,)),
        dma((NZ,)),
        dma,
        dma,
        dma,
    ]
    parts = pl.pallas_call(
        kernel,
        out_shape=(
            jax.ShapeDtypeStruct((TOK, WIDTH), BF16),
            jax.ShapeDtypeStruct((NT, WIDTH, WIDTH), F32),
            jax.ShapeDtypeStruct((NT, WIDTH, 2 * RANK), BF16),
            jax.ShapeDtypeStruct((2, 2 * RANK, WIDTH), BF16),
        ),
        in_specs=[hbm] * 5,
        out_specs=(vmem,) * 4,
        scratch_shapes=scratch,
        compiler_params=pltpu.CompilerParams(
            collective_id=0, has_side_effects=True, vmem_limit_bytes=32 * 1024 * 1024
        ),
    )(*(
        pltpu.with_memory_space_constraint(v, pltpu.HBM)
        for v in (acts, grads_out, weight, basis_init, feedback)
    ))
    input_grads, total, factor_t, coefs = parts
    return pl.pallas_call(
        finish,
        out_shape=(
            jax.ShapeDtypeStruct((TOK, WIDTH), BF16),
            jax.ShapeDtypeStruct((1, D, WIDTH), BF16),
            jax.ShapeDtypeStruct((ROWS, WIDTH), F32),
        ),
        in_specs=[vmem] * 4,
        out_specs=(hbm,) * 3,
        scratch_shapes=[
            pltpu.VMEM((NT, WIDTH, WIDTH), BF16),
            pltpu.VMEM((ROWS, WIDTH), F32),
            dma((NT + 2,)),
        ],
        compiler_params=pltpu.CompilerParams(vmem_limit_bytes=20 * 1024 * 1024),
    )(total, factor_t, coefs, input_grads)


def solution(mesh):
    return jax.shard_map(
        local,
        mesh=mesh,
        in_specs=(
            P("dp", "tensor"),
            P("dp", "tensor"),
            P("dp", "tensor"),
            P(None, "tensor"),
            P("dp", None, "tensor"),
        ),
        out_specs=(P("dp", "tensor"), P("dp", None, "tensor"), P("dp", "tensor")),
        check_vma=False,
    )
```

```python
import jax
import jax.numpy as jnp
from jax import lax
from jax.experimental import pallas as pl
from jax.experimental.pallas import tpu as pltpu
from jax.sharding import PartitionSpec as P

MESH = pl.DeviceIdType.MESH
F32 = jnp.float32
BF16 = jnp.bfloat16
RANK = 64
TOK = 128
WIDTH = 384
NT = 8
NX, NZ, NC = 4, 8, 2
ROWS = 48
D = NT * WIDTH

NN = (((1,), (0,)), ((), ()))
NTD = (((1,), (1,)), ((), ()))
TN = (((0,), (0,)), ((), ()))


def mm(a, b, dims):
    return lax.dot_general(a, b, dims, preferred_element_type=F32)


def mm32(a, b, dims):
    return lax.dot_general(
        a, b, dims, precision=lax.Precision.HIGHEST, preferred_element_type=F32
    )


def pieces(value, n):
    parts = []
    for _ in range(n):
        top = value.astype(BF16)
        parts.append(top)
        value = value - top.astype(F32)
    return jnp.concatenate(parts, axis=0)


def folded(stack, n):
    rows = stack.shape[0] // n
    total = stack[(n - 1) * rows :]
    for i in range(n - 2, -1, -1):
        total = total + stack[i * rows : (i + 1) * rows]
    return total


def eliminate(a, first, last):
    rows = lax.broadcasted_iota(jnp.int32, (RANK, 1), 0)
    for j in range(first, last):
        scaled = a[j : j + 1, :] / a[j : j + 1, j : j + 1]
        column = jnp.where(rows > j, a[:, j : j + 1], 0.0)
        a = a - column * scaled
    return a


def kernel(
    acts_hbm, grads_hbm, weight_hbm, basis_hbm, fb_hbm,
    ig_out, t0, ft, coefs,
    grads, weight, basis, fb, acts_all, grads_all, wbuf, fp, rc, f1, rx, f2, rz, rzx, f_all,
    sp, rs, rsz, sfull, through, direct, work, steps,
    in_sem,
    sent, ring_r, gr_r, spread, wz_r, wx_r, wy_r, wc_r,
    fc_r, fx_r, fz_r, zx_r, az_r, ax_r, ac_r, sx_r, sz_r, sa_r,
):
    dp = lax.axis_index("dp")
    y = lax.axis_index("tensor")
    c = dp % NC
    z = (dp // NC) % NZ
    x = dp // (NC * NZ)

    def at(x_, z_, c_):
        return (x_ * NZ + z_) * NC + c_

    q = c * NX + x
    group = dp // NT
    pair = (y * NT + dp % NT, group)
    y_peers = [(dp, (y + k) % NT) for k in range(1, NT)]
    z_peers = [(at(x, (z + k) % NZ, c), y) for k in range(1, NZ)]
    xc_peers = [
        (at((x + (o % NX)) % NX, z, (c + o // NX) % NC), y) for o in range(1, NX * NC)
    ]
    partner = xc_peers[NX - 1]
    x_peers = xc_peers[: NX - 1]
    swaps = group != y

    sends = []

    def arrived(ref, rsem):
        pltpu.make_async_copy(ref, ref, rsem).wait()

    def send(src, dst, rsem, peer):
        cp = pltpu.make_async_remote_copy(
            src_ref=src, dst_ref=dst, send_sem=sent, recv_sem=rsem,
            device_id=peer, device_id_type=MESH,
        )
        cp.start()
        sends.append(cp)
        return cp

    def fence():
        @pl.when(dp >= 0)
        def _():
            steps[0] = 1

    barrier = pltpu.get_barrier_semaphore()
    for peer in [y_peers[0], y_peers[NT - 2]] + z_peers + xc_peers:
        pl.semaphore_signal(barrier, inc=1, device_id=peer, device_id_type=MESH)

    @pl.when(swaps)
    def _():
        pl.semaphore_signal(barrier, inc=1, device_id=pair, device_id_type=MESH)

    loads = [
        pltpu.make_async_copy(src, dst, in_sem.at[i])
        for i, (src, dst) in enumerate([
            (acts_hbm, acts_all.at[y]), (weight_hbm, weight), (grads_hbm, grads),
            (basis_hbm, basis),
            (fb_hbm.at[0], fb),
        ])
    ]
    for cp in loads:
        cp.start()
    fence()
    loads[0].wait()
    loads[1].wait()
    fence()
    pl.semaphore_wait(barrier, 16 + jnp.where(swaps, 1, 0))

    fence()
    mine = wbuf.at[group, z % 4, c]
    swap = pltpu.make_async_remote_copy(
        src_ref=weight, dst_ref=wbuf.at[y, z % 4, c], send_sem=spread.at[0], recv_sem=spread.at[1],
        device_id=pair, device_id_type=MESH,
    )

    @pl.when(swaps)
    def _():
        swap.start()

    @pl.when(jnp.logical_not(swaps))
    def _():
        wbuf[y, z % 4, c] = weight[...]

    right = (dp, (y + 1) % NT)
    left = (dp, (y + NT - 1) % NT)
    quarter = TOK // 4

    def block_of(k, way):
        return (y - k + NT) % NT if way == 0 else (y + k) % NT

    def ring(way, k, h, peer):
        part = acts_all.at[block_of(k, way), pl.ds(h * quarter, quarter)]
        return send(part, part, ring_r.at[way, k, h], peer)

    hops = {}
    for h in range(4):
        hops[0, 0, h] = ring(0, 0, h, right)
        hops[1, 0, h] = ring(1, 0, h, left)

    fence()
    loads[2].wait()
    loads[3].wait()
    grads_all[y] = grads[...]
    bs = pieces(basis[...], 3)
    hs = pieces(folded(mm(bs, grads[...], NTD), 3), 3)
    fence()
    loads[4].wait()
    for t in range(NT):
        fp[t] = folded(mm(bs, fb[t * WIDTH : (t + 1) * WIDTH], NTD), 3)
    core_cp = {}

    def add_acts(k, way):
        t = block_of(k, way)
        fp[t] = fp[t] + folded(mm(hs, acts_all[t], NN), 3)
        core_cp[k, way] = send(
            fp.at[t, pl.ds(32 * (1 - c), 32)], rc.at[t], fc_r.at[t], partner
        )

    def x_stage(k, way):
        t = block_of(k, way)
        core_cp[k, way].wait_recv()
        f1[t] = fp[t, pl.ds(pl.multiple_of(32 * c, 32), 32)] + rc[t]
        for d in range(1, NX):
            to = (x + d) % NX
            send(
                f1.at[t, pl.ds(pl.multiple_of(8 * to, 8), 8)], rx.at[t, d - 1],
                fx_r.at[t], x_peers[d - 1],
            )

    own = pl.ds(pl.multiple_of(8 * x, 8), 8)

    def z_copy(t, away):
        return pltpu.make_async_remote_copy(
            src_ref=f2.at[t], dst_ref=rz.at[away - 1], send_sem=sent,
            recv_sem=fz_r, device_id=(at(x, t, c), y), device_id_type=MESH,
        )

    def back_copy(t, i):
        return pltpu.make_async_remote_copy(
            src_ref=f_all.at[t, q], dst_ref=f_all.at[t, q], send_sem=sent,
            recv_sem=az_r.at[t], device_id=z_peers[i], device_id_type=MESH,
        )

    def x_sum(t):
        arrived(rx.at[t], fx_r.at[t])
        return f1[t, own] + rx[t, 0] + rx[t, 1] + rx[t, 2]

    def z_stage(k, way):
        t = block_of(k, way)
        f2[t] = x_sum(t)
        away = (t - z + NZ) % NZ

        @pl.when(away != 0)
        def _():
            z_copy(t, away).start()

    def keep(t, f3):
        top = f3.astype(BF16).astype(F32)
        f_all[t, q] = jnp.concatenate([top, f3 - top], axis=0).astype(BF16)

    def owner_stage(k, way):
        t = block_of(k, way)

        @pl.when(t == z)
        def _():
            arrived(rz, fz_r)
            f3 = f2[t]
            for i in range(NZ - 1):
                f3 = f3 + rz[i]
            keep(t, f3)
            for i in range(NZ - 1):
                back_copy(t, i).start()

    def back_x_sends(t):
        for i in range(NX - 1):
            send(f_all.at[t, q], f_all.at[t, q], ax_r.at[t], x_peers[i])

    def back_x(k, way):
        t = block_of(k, way)

        @pl.when(t != z)
        def _():
            arrived(f_all.at[t, q], az_r.at[t])

        back_x_sends(t)

    def last_z_stage():
        rzx[z] = x_sum(block_of(4, 0))
        for i in range(NZ - 1):
            send(rzx.at[z], rzx.at[z], zx_r, z_peers[i])

    def last_back_x():
        arrived(rzx.at[pl.ds(0, NZ - 1)], zx_r)
        f3 = rzx[0]
        for i in range(1, NZ):
            f3 = f3 + rzx[i]
        keep(block_of(4, 0), f3)
        back_x_sends(block_of(4, 0))

    back_core = {}

    def back_core_stage(k, way):
        t = block_of(k, way)
        arrived(f_all.at[t, pl.ds(0, NX - 1)], ax_r.at[t])
        part = f_all.at[t, pl.ds(NX * c, NX)]
        back_core[k, way] = send(part, part, ac_r.at[t], partner)

    through[...] = jnp.zeros((2 * RANK, TOK), F32)
    direct[...] = jnp.zeros((2 * RANK, WIDTH), F32)

    def second_part(which):
        for key in which:
            back_core[key].wait_recv()
        acts_part, own_part = through[...], direct[...]
        for key in which:
            t = block_of(*key)
            block = f_all[t].reshape(2 * RANK, WIDTH)
            rows = pl.ds(pl.multiple_of(t * WIDTH, WIDTH), WIDTH)
            acts_part = acts_part + mm(block, acts_all[t], NTD)
            own_part = own_part + mm(block, fb[rows], NN)
        through[...], direct[...] = acts_part, own_part

    ways = {0: [0], 1: [0, 1], 2: [0, 1], 3: [0, 1], 4: [0]}

    def each(stage, k):
        for way in ways[k]:
            stage(k, way)

    for k in range(5):
        if k == 4:
            fence()
            each(x_stage, 3)
            each(z_stage, 1)
        fence()
        if k:
            for h in range(4):
                for way, peer in ((0, right), (1, left)):
                    if (way, k - 1, h) in hops:
                        hops[way, k - 1, h].wait_recv()
                        if k < 3 or (k == 3 and h // 2 == way):
                            hops[way, k, h] = ring(way, k, h, peer)
        fence()
        each(add_acts, k)
        fence()
        if 1 <= k < 4:
            each(x_stage, k - 1)
        fence()
        if k == 2:
            @pl.when(swaps)
            def _():
                swap.wait_recv()
            for i in range(NZ - 1):
                send(mine, mine, wz_r, z_peers[i])
        fence()
        if k == 3:
            each(z_stage, 0)

    fence()
    each(x_stage, 4)
    for i in range(NT - 1):
        send(grads, grads_all.at[y], gr_r, y_peers[i])
    fence()
    each(owner_stage, 0)
    fence()
    each(z_stage, 2)
    fence()
    each(z_stage, 3)
    fence()
    arrived(wbuf.at[0:NZ - 1, 0, 0], wz_r)
    piece = wbuf.at[pl.ds(2 * x, 2), :, c]
    wx = [
        send(piece, piece, wx_r.at[way], x_peers[(0, NX - 2)[way]]) for way in (0, 1)
    ]
    fence()
    last_z_stage()
    fence()
    for t in range(NT):
        t0[t] = mm(acts_all[t], grads[...], TN) + fb[t * WIDTH : (t + 1) * WIDTH].astype(F32)
    fence()
    each(owner_stage, 1)
    fence()
    each(back_x, 0)
    fence()
    each(owner_stage, 2)
    fence()
    each(owner_stage, 3)
    fence()
    each(back_x, 1)
    fence()
    last_back_x()
    fence()
    each(back_x, 2)
    fence()
    each(back_core_stage, 0)
    each(back_core_stage, 1)
    fence()
    each(back_x, 3)
    fence()
    each(back_core_stage, 2)
    fence()
    second_part([(0, 0), (1, 0), (1, 1)])
    fence()
    each(back_core_stage, 4)
    each(back_core_stage, 3)
    fence()
    second_part([(2, 0), (2, 1)])
    fence()
    second_part([(4, 0), (3, 0), (3, 1)])

    def unpaired(pairs):
        v = pairs.reshape(RANK // 8, 2, 8, pairs.shape[1])
        return (v[:, 0] + v[:, 1]).reshape(RANK, pairs.shape[1])

    fence()
    local = unpaired(direct[...]) + folded(mm(pieces(unpaired(through[...]), 3), grads[...], NN), 3)
    sp[...] = local.reshape(RANK // 8, 8, WIDTH)
    for o in range(1, NX * NC):
        to = ((c + o // NX) % NC) * NX + (x + o % NX) % NX
        send(sp.at[to], rs.at[o - 1], sx_r, xc_peers[o - 1])

    fence()
    wy = []
    for way in (0, 1):
        wx[way].wait_recv()
        piece = wbuf.at[2 * ((x + (NX - 1, 1)[way]) % NX) + way, :, c]
        wy.append(send(piece, piece, wy_r.at[way], x_peers[(0, NX - 2)[way]]))
    fence()
    gram = jnp.zeros((2 * RANK, 2 * RANK), F32)
    for t in range(NT):
        block = f_all[t].reshape(2 * RANK, WIDTH)
        gram = gram + mm(block, block, NTD)
    lanes = lax.broadcasted_iota(jnp.int32, (2 * RANK, RANK), 0)
    cols = lax.broadcasted_iota(jnp.int32, (2 * RANK, RANK), 1)
    pick = jnp.where((lanes // 16) * 8 + lanes % 8 == cols, 1.0, 0.0)
    gram = mm32(unpaired(gram), pick, NN)
    eye = jnp.where(
        lax.broadcasted_iota(jnp.int32, (RANK, RANK), 0)
        == lax.broadcasted_iota(jnp.int32, (RANK, RANK), 1), 1.0, 0.0,
    )
    work[...] = jnp.concatenate([gram, eye], axis=1)
    fence()
    work[...] = eliminate(work[...], 0, 12)

    fence()
    arrived(rs, sx_r)
    s1 = sp[q]
    for i in range(NX * NC - 1):
        s1 = s1 + rs[i]
    rsz[z] = s1
    for i in range(NZ - 1):
        send(rsz.at[z], rsz.at[z], sz_r, z_peers[i])
    fence()
    work[...] = eliminate(work[...], 12, 44)
    fence()
    arrived(rsz.at[pl.ds(0, NZ - 1)], sz_r)
    fence()
    for cp in wy:
        cp.wait_recv()
    whalf = wbuf.at[:, :, c]
    wc = send(whalf, whalf, wc_r, partner)
    fence()
    s2 = rsz[0]
    for i in range(1, NZ):
        s2 = s2 + rsz[i]
    sfull[q] = s2
    for i in range(NX * NC - 1):
        send(sfull.at[q], sfull.at[q], sa_r, xc_peers[i])
    fence()
    work[...] = eliminate(work[...], 44, RANK)
    fence()
    for t in range(NT):
        columns = f_all[t].reshape(2 * RANK, WIDTH).astype(F32).T.astype(BF16)
        ft[t] = jnp.concatenate([columns, columns], axis=1)
    fence()
    arrived(grads_all.at[pl.ds(0, NT - 1)], gr_r)
    wc.wait_recv()
    fence()
    out = jnp.zeros((TOK, WIDTH), F32)
    for j in range(NT):
        out = out + mm(grads_all[j], wbuf[j].reshape(WIDTH, WIDTH), NTD)
    ig_out[...] = out.astype(BF16)

    fence()
    arrived(sfull.at[pl.ds(0, NX * NC - 1)], sa_r)

    fence()
    pivots = jnp.sum(work[:, :RANK] * eye, axis=1, keepdims=True)
    inverse = work[:, RANK:]
    solved = mm32(inverse, sfull[...].reshape(RANK, WIDTH), NN) / (pivots * 64.0)
    coef = mm32(inverse, solved, TN)
    ctop = coef.astype(BF16).astype(F32)

    def doubled(v):
        v = v.reshape(RANK // 8, 1, 8, WIDTH)
        return jnp.concatenate([v, v], axis=1).reshape(2 * RANK, WIDTH).astype(BF16)

    coefs[...] = jnp.concatenate([doubled(ctop), doubled(coef - ctop)], axis=0)

    fence()
    for cp in sends:
        cp.wait_send()
    for t in [block_of(k, way) for k in range(4) for way in ways[k]]:
        @pl.when(t != z)
        def _():
            z_copy(t, (t - z + NZ) % NZ).wait_send()

        @pl.when(t == z)
        def _():
            for i in range(NZ - 1):
                back_copy(t, i).wait_send()

    @pl.when(swaps)
    def _():
        swap.wait_send()


def finish(t0, ft, coefs, ig, ig_out, nf_out, up_out, nf, up, sems):
    def low_rank(left_side):
        return mm(left_side, coefs[...], NN)

    stores = [pltpu.make_async_copy(ig, ig_out, sems.at[NT])]
    stores[0].start()
    dp = lax.axis_index("dp")
    first = pl.multiple_of((dp % NT) * ROWS, 16)
    up[...] = low_rank(ft[dp // NT, pl.ds(first, ROWS)])
    stores.append(pltpu.make_async_copy(up, up_out, sems.at[NT + 1]))
    stores[1].start()
    for t in range(NT):
        nf[t] = (t0[t] - low_rank(ft[t])).astype(BF16)
        stores.append(
            pltpu.make_async_copy(nf.at[t], nf_out.at[0, pl.ds(t * WIDTH, WIDTH)], sems.at[t])
        )
        stores[-1].start()
    for cp in stores:
        cp.wait()


def local(acts, grads_out, weight, basis_init, feedback):
    vmem = pl.BlockSpec(memory_space=pltpu.VMEM)
    hbm = pl.BlockSpec(memory_space=pltpu.HBM)
    dma = pltpu.SemaphoreType.DMA
    scratch = [
        pltpu.VMEM((TOK, WIDTH), BF16),
        pltpu.VMEM((ROWS, WIDTH), BF16),
        pltpu.VMEM((RANK, WIDTH), F32),
        pltpu.VMEM((D, WIDTH), BF16),
        pltpu.VMEM((NT, TOK, WIDTH), BF16),
        pltpu.VMEM((NT, TOK, WIDTH), BF16),
        pltpu.VMEM((NT, 4, NC, ROWS, WIDTH), BF16),
        pltpu.VMEM((NT, RANK, WIDTH), F32),
        pltpu.VMEM((NT, RANK // 2, WIDTH), F32),
        pltpu.VMEM((NT, RANK // 2, WIDTH), F32),
        pltpu.VMEM((NT, NX - 1, 8, WIDTH), F32),
        pltpu.VMEM((NT, 8, WIDTH), F32),
        pltpu.VMEM((NZ - 1, 8, WIDTH), F32),
        pltpu.VMEM((NZ, 8, WIDTH), F32),
        pltpu.VMEM((NT, NX * NC, 16, WIDTH), BF16),
        pltpu.VMEM((NX * NC, 8, WIDTH), F32),
        pltpu.VMEM((NX * NC - 1, 8, WIDTH), F32),
        pltpu.VMEM((NZ, 8, WIDTH), F32),
        pltpu.VMEM((NX * NC, 8, WIDTH), F32),
        pltpu.VMEM((2 * RANK, TOK), F32),
        pltpu.VMEM((2 * RANK, WIDTH), F32),
        pltpu.VMEM((RANK, 2 * RANK), F32),
        pltpu.SMEM((1,), jnp.int32),
        dma((5,)),
        dma,
        dma((2, 4, 4)),
        dma,
        dma((2,)),
        dma,
        dma((2,)),
        dma((2,)),
        dma,
        dma((NT,)),
        dma((NT,)),
        dma,
        dma,
        dma((NZ,)),
        dma((NZ,)),
        dma((NZ,)),
        dma,
        dma,
        dma,
    ]
    parts = pl.pallas_call(
        kernel,
        out_shape=(
            jax.ShapeDtypeStruct((TOK, WIDTH), BF16),
            jax.ShapeDtypeStruct((NT, WIDTH, WIDTH), F32),
            jax.ShapeDtypeStruct((NT, WIDTH, 4 * RANK), BF16),
            jax.ShapeDtypeStruct((4 * RANK, WIDTH), BF16),
        ),
        in_specs=[hbm] * 5,
        out_specs=(vmem,) * 4,
        scratch_shapes=scratch,
        compiler_params=pltpu.CompilerParams(
            collective_id=0, has_side_effects=True, vmem_limit_bytes=32 * 1024 * 1024
        ),
    )(*(
        pltpu.with_memory_space_constraint(v, pltpu.HBM)
        for v in (acts, grads_out, weight, basis_init, feedback)
    ))
    input_grads, total, factor_t, coefs = parts
    return pl.pallas_call(
        finish,
        out_shape=(
            jax.ShapeDtypeStruct((TOK, WIDTH), BF16),
            jax.ShapeDtypeStruct((1, D, WIDTH), BF16),
            jax.ShapeDtypeStruct((ROWS, WIDTH), F32),
        ),
        in_specs=[vmem] * 4,
        out_specs=(hbm,) * 3,
        scratch_shapes=[
            pltpu.VMEM((NT, WIDTH, WIDTH), BF16),
            pltpu.VMEM((ROWS, WIDTH), F32),
            dma((NT + 2,)),
        ],
        compiler_params=pltpu.CompilerParams(vmem_limit_bytes=20 * 1024 * 1024),
    )(total, factor_t, coefs, input_grads)


def solution(mesh):
    return jax.shard_map(
        local,
        mesh=mesh,
        in_specs=(
            P("dp", "tensor"),
            P("dp", "tensor"),
            P("dp", "tensor"),
            P(None, "tensor"),
            P("dp", None, "tensor"),
        ),
        out_specs=(P("dp", "tensor"), P("dp", None, "tensor"), P("dp", "tensor")),
        check_vma=False,
    )
```
